256 devices in a mesh: sta: 8 (over z), win: 32 (over y, x, core).
Axes of the slice: x: 4, y: 4, z: 8, core: 2. Of those that a mesh axis runs over, the one named last changes fastest.
Arguments:
- traces: float32 [1024, 32, 8192], P('sta', 'win')
- pair_blocks: int32 [8, 2], P('sta'), may hold values from 0 to 15, as said below
Outputs:
- correlations: float32 [64, 8, 64, 512], P('win', 'sta')
The draws below stay inside these ranges and needn't reach their ends.
Inputs may be any that keep to these rules, and one draw needn't show every extreme that they name: pair_blocks[p, 0] <= pair_blocks[p, 1] <= pair_blocks[p, 0] + 2; pairs per first block are uneven.
All inputs are finite; a program needn't handle non-finite values.
Results may differ from the reference program's by a relative error of at most 0.0017.
Values may be sent and summed in bfloat16 or wider, within the bound.
A program may use at most 64 MiB of HBM per device.

```python
import math
import jax
import jax.numpy as jnp
from jax import lax

PAIR_DEV = 1
L = 8192
BLOCK = 64
LAGS = 512
K0 = 256
STATIONS = 1024
WINDOWS = 32
BANDS = 512
NBLK = 16
NPAIR = 8


def draw_traces(key, part):
    key = jax.random.fold_in(key, 11)
    key_amp, key_noise = jax.random.split(key, 2)
    amp = jnp.exp(jax.random.uniform(key_amp, (STATIONS, WINDOWS, 1), jnp.float32, 0.0, jnp.log(10.0)))
    noise = jax.random.normal(key_noise, (STATIONS, WINDOWS, L), jnp.float32)
    return amp * noise


def draw_pair_blocks(key, part):
    key = jax.random.fold_in(key, 23)
    key_first, key_gap = jax.random.split(key)
    owners = NPAIR // PAIR_DEV
    per_owner = NBLK // owners
    first = jax.random.randint(key_first, (NPAIR,), 0, NBLK, jnp.int32)
    gap = jax.random.randint(key_gap, (NPAIR,), 0, 3, jnp.int32)
    first = first.at[0].set(NBLK - 1)
    gap = gap.at[0].set(0)
    far_block = (1 + owners // 2) % owners * per_owner
    first = first.at[PAIR_DEV].set(far_block)
    first = first.at[NPAIR // 2].set(0)
    second = jnp.minimum(first + gap, NBLK - 1)
    second = second.at[NPAIR - 1].set(jnp.maximum(first[NPAIR - 1], NBLK - 1))
    first = first.at[NPAIR - 1].set(jnp.maximum(first[NPAIR - 1], NBLK - 3))
    return jnp.stack([first, second], axis=1)


def setup_inputs(seed: int = 0) -> dict:
    key_of = jax.random.split(jax.random.key(seed), 3)
    traces = draw_traces(jax.random.fold_in(key_of[2], 71), 0)
    pair_blocks = draw_pair_blocks(jax.random.fold_in(key_of[2], 71), 0)
    return {"traces": traces, "pair_blocks": pair_blocks}


def lag_tables(first_bin, count):
    freqs = first_bin + jnp.arange(count, dtype=jnp.int32)
    shifts = (jnp.arange(LAGS, dtype=jnp.int32) - LAGS // 2) % L
    phase = freqs[:, None] * shifts[None, :] % L
    angle = phase.astype(jnp.float32) * (2.0 * math.pi / L)
    return (jnp.cos(angle), jnp.sin(angle))

def reference(traces, pair_blocks):
    spectrum = jnp.fft.rfft(traces, axis=-1)[:, :, K0:K0 + BANDS]
    real_part = jnp.real(spectrum)
    imag_part = jnp.imag(spectrum)
    power = lax.optimization_barrier(jnp.mean(real_part * real_part + imag_part * imag_part, axis=-1, keepdims=True))
    scale = jnp.sqrt(power + 1e-06)
    white = jnp.stack([(real_part / scale).astype(jnp.bfloat16), (imag_part / scale).astype(jnp.bfloat16)])
    cos_table, sin_table = lag_tables(K0, BANDS)
    norm = float(WINDOWS * BANDS) ** (-0.5)

    def one_pair(pair):
        first = lax.dynamic_slice_in_dim(white, (pair[0] * BLOCK).astype(jnp.int32), BLOCK, 1)
        second = lax.dynamic_slice_in_dim(white, (pair[1] * BLOCK).astype(jnp.int32), BLOCK, 1)
        left = jnp.concatenate([first[0], first[1]], axis=0).astype(jnp.float32)
        right = jnp.concatenate([second[0], second[1]], axis=0).astype(jnp.float32)
        prod = jnp.einsum('awf,bwf->fab', left, right, precision=lax.Precision.HIGHEST)
        cross_re = prod[:, :BLOCK, :BLOCK] + prod[:, BLOCK:, BLOCK:]
        cross_im = prod[:, BLOCK:, :BLOCK] - prod[:, :BLOCK, BLOCK:]
        lagged = jnp.einsum('fij,ft->ijt', cross_re, cos_table, precision=lax.Precision.HIGHEST)
        lagged = lagged - jnp.einsum('fij,ft->ijt', cross_im, sin_table, precision=lax.Precision.HIGHEST)
        return lagged * norm
    stacked = lax.map(one_pair, pair_blocks)
    return jnp.transpose(stacked, (1, 0, 2, 3))
```

```python
import functools
import math

import jax
import jax.numpy as jnp
import ml_dtypes
import numpy as np
from jax import lax
from jax.experimental import pallas as pl
from jax.experimental.pallas import tpu as pltpu
from jax.sharding import PartitionSpec as P

L = 8192
LAGS = 512
K0 = 256
BANDS = 512
STA = 8
WIN = 32
ST = 128
SEG = 64
RADIX = 16
FOLD = L // RADIX
MESH = pl.DeviceIdType.MESH


def bin_of():
    bins = np.zeros((WIN, STA, 2), np.int64)
    for z in range(STA):
        for q in range(1, 8):
            for u in range(4):
                m = 16 + 4 * z + u
                bins[4 * (q - 1) + u, z] = (16 * m + q, 16 * m + 16 - q)
        for half in range(2):
            for u in range(2):
                for s in range(2):
                    bins[28 + 2 * half + u, z, s] = 16 * (16 + 4 * z + 2 * u + s) + 8 * half
    return bins


def split(table):
    high = table.astype(ml_dtypes.bfloat16)
    low = (table - high.astype(np.float64)).astype(ml_dtypes.bfloat16)
    return high, low


@functools.cache
def tables():
    bins = bin_of()
    n = np.arange(FOLD)

    def trig(k):
        angle = 2 * math.pi * ((k * n) % L) / L
        return np.cos(angle), np.sin(angle)

    odd = np.zeros((7, 4, STA, 2, 2, 2 * FOLD))
    for q in range(1, 8):
        for u in range(4):
            for z in range(STA):
                for s in range(2):
                    c, d = trig(bins[4 * (q - 1) + u, z, s])
                    sign = 1.0 if s == 0 else -1.0
                    odd[q - 1, u, z, s, 0] = np.concatenate([c, sign * d])
                    odd[q - 1, u, z, s, 1] = np.concatenate([-d, sign * c])
    even = np.zeros((2, 2, STA, 2, 2, FOLD))
    for half in range(2):
        for u in range(2):
            for z in range(STA):
                for s in range(2):
                    c, d = trig(bins[28 + 2 * half + u, z, s])
                    even[half, u, z, s, 0] = c
                    even[half, u, z, s, 1] = -d
    shifts = (np.arange(LAGS) - LAGS // 2) % L
    angle = 2 * math.pi * ((bins[..., None] * shifts) % L) / L
    lag = np.stack([np.cos(angle), -np.sin(angle)], axis=3)
    lag = lag.reshape(2 * BANDS, LAGS).T * float(WIN * BANDS) ** (-0.5)
    odd = np.stack(split(odd.reshape(7, 128, 2 * FOLD)), axis=1)
    even = np.stack(split(even.reshape(2, 64, FOLD)), axis=1)
    lag = np.concatenate(split(lag), axis=0)
    return odd, even, lag


def fold16(x):
    r2 = math.sqrt(0.5)
    c1 = math.cos(math.pi / 8)
    c3 = math.sin(math.pi / 8)
    e = [x[a] + x[a + 8] for a in range(8)]
    o = [x[a] - x[a + 8] for a in range(8)]
    f = [e[a] + e[a + 4] for a in range(4)]
    g = [e[a] - e[a + 4] for a in range(4)]
    f02, f13 = f[0] + f[2], f[1] + f[3]
    gd, gs = r2 * (g[1] - g[3]), r2 * (g[1] + g[3])
    d = [None] + [o[a] - o[8 - a] for a in range(1, 4)]
    s = [None] + [o[a] + o[8 - a] for a in range(1, 4)]
    d2, s2 = r2 * d[2], r2 * s[2]
    p, m = o[0] + d2, o[0] - d2
    u, v = c1 * d[1] + c3 * d[3], c3 * d[1] - c1 * d[3]
    pp, mm = s2 + o[4], s2 - o[4]
    uu, vv = c3 * s[1] + c1 * s[3], c1 * s[1] - c3 * s[3]
    real = [f02 + f13, p + u, g[0] + gd, m + v, f[0] - f[2], m - v, g[0] - gd, p - u, f02 - f13]
    imag = [None, -(uu + pp), -(g[2] + gs), -(vv + mm), f[3] - f[1], mm - vv, g[2] - gs, pp - uu]
    return real, imag


def kernel(
    x_ref, pair_ref, odd_ref, even_ref, lag_ref, out_ref,
    x_v, odd_v, even_v, lag_v, pairs, fodd, feven, spec,
    asend, arecv, bsend, brecv, csend, crecv, dsend, drecv, order,
    x_sem, t_sem, p_ssem, p_rsem, a_ssem, a_rsem, b_ssem, b_rsem, c_ssem, c_rsem, d_ssem, d_rsem,
):
    me_s = lax.axis_index("sta")
    me_w = lax.axis_index("win")

    x_copies = [
        pltpu.make_async_copy(x_ref.at[pl.ds(2048 * i, 2048)], x_v.at[pl.ds(2048 * i, 2048)], x_sem.at[i])
        for i in range(4)
    ]
    t_copies = [
        pltpu.make_async_copy(src, dst, t_sem.at[i])
        for i, (src, dst) in enumerate(((odd_ref, odd_v), (even_ref, even_v), (lag_ref, lag_v)))
    ]
    for copy in x_copies + t_copies:
        copy.start()

    barrier = pltpu.get_barrier_semaphore()

    def greet(axis, me, count):
        def step(i, _):
            peer = lax.rem(me + i, count)
            pl.semaphore_signal(barrier, inc=1, device_id={axis: peer}, device_id_type=MESH)
            return 0

        lax.fori_loop(1, count, step, 0)

    greet("sta", me_s, STA)
    greet("win", me_w, WIN)

    for chunk in range(4):
        x_copies[chunk].wait()

        def fold(t, _, chunk=chunk):
            lane_tile = lax.rem(t, 4)
            i2 = t // 4
            first = chunk * 2048 + i2 * 64
            x = [x_v[pl.ds(first + 4 * a + lane_tile, 16, stride=128), :] for a in range(RADIX)]
            real, imag = fold16(x)
            row = pl.multiple_of((chunk // 2) * 64 + i2 * 32 + (chunk % 2) * 16, 16)
            lane = pl.multiple_of(lane_tile * 128, 128)

            def put(dst, at, value):
                high = value.astype(jnp.bfloat16)
                low = (value - high.astype(jnp.float32)).astype(jnp.bfloat16)
                dst[pl.ds(row, 16), pl.ds(at, 128)] = high
                dst[pl.ds(row + 128, 16), pl.ds(at, 128)] = low

            put(feven.at[0], lane, real[0])
            put(feven.at[1], lane, real[8])
            for q in range(1, 8):
                put(fodd.at[q - 1], lane, real[q])
                put(fodd.at[q - 1], pl.multiple_of(lane + FOLD, 128), imag[q])
            return 0

        lax.fori_loop(0, 8, fold, 0)

    contract_last = (((1,), (1,)), ((), ()))

    def dft(table, data):
        high = lax.dot_general(table[0], data, contract_last, preferred_element_type=jnp.float32)
        low = lax.dot_general(table[1], data[:ST], contract_last, preferred_element_type=jnp.float32)
        return high[:, :ST] + (high[:, ST:] + low)

    t_copies[0].wait()

    def odd_class(q, power):
        value = dft(odd_v[q], fodd[q])
        spec[pl.ds(pl.multiple_of(q * 128, 128), 128), :] = value
        return power + jnp.sum((value * value).reshape(16, 8, ST), axis=0)

    power = lax.fori_loop(0, 7, odd_class, jnp.zeros((8, ST), jnp.float32))
    t_copies[1].wait()
    for half in range(2):
        value = dft(even_v[half], feven[half])
        spec[896 + 64 * half : 960 + 64 * half, :] = value
        power = power + jnp.sum((value * value).reshape(8, 8, ST), axis=0)
    mean = jnp.sum(power, axis=0, keepdims=True) * (1.0 / BANDS)
    inverse = 1.0 / jnp.sqrt(mean + 1e-06)
    for i in range(WIN):
        asend[i] = (spec[32 * i : 32 * i + 32, :] * inverse).astype(jnp.bfloat16)

    pl.semaphore_wait(barrier, STA - 1 + WIN - 1)

    def p_copy(peer, slot):
        return pltpu.make_async_remote_copy(
            src_ref=pair_ref, dst_ref=pairs.at[slot], send_sem=p_ssem.at[peer], recv_sem=p_rsem.at[slot],
            device_id={"sta": peer}, device_id_type=MESH,
        )

    def a_copy(peer, slot):
        return pltpu.make_async_remote_copy(
            src_ref=asend.at[peer], dst_ref=arecv.at[slot], send_sem=a_ssem.at[peer], recv_sem=a_rsem.at[slot],
            device_id={"win": peer}, device_id_type=MESH,
        )

    def b_copy(peer, slot):
        return pltpu.make_async_remote_copy(
            src_ref=bsend.at[peer], dst_ref=brecv.at[slot], send_sem=b_ssem.at[peer], recv_sem=b_rsem.at[slot],
            device_id={"sta": peer}, device_id_type=MESH,
        )

    def c_copy(peer, slot):
        return pltpu.make_async_remote_copy(
            src_ref=csend.at[peer], dst_ref=crecv.at[slot], send_sem=c_ssem.at[peer], recv_sem=c_rsem.at[slot],
            device_id={"sta": peer}, device_id_type=MESH,
        )

    def d_copy(peer, slot):
        return pltpu.make_async_remote_copy(
            src_ref=dsend.at[peer], dst_ref=drecv.at[slot], send_sem=d_ssem.at[peer], recv_sem=d_rsem.at[slot],
            device_id={"win": peer}, device_id_type=MESH,
        )

    def each(count, me, action):
        def step(i, _):
            action(lax.rem(me + i, count))
            return 0

        lax.fori_loop(1, count, step, 0)

    each(WIN, me_w, lambda peer: a_copy(peer, me_w).start())
    each(STA, me_s, lambda peer: p_copy(peer, me_s).start())
    arecv[me_w] = asend[me_w]
    pairs[me_s, 0, 0] = pair_ref[0, 0]
    pairs[me_s, 0, 1] = pair_ref[0, 1]
    each(WIN, me_w, lambda peer: a_copy(peer, peer).wait_recv())

    for z in range(STA):
        bsend[z] = jnp.swapaxes(arecv[:, 4 * z : 4 * z + 4, :], 0, 1)
    each(STA, me_s, lambda peer: b_copy(peer, me_s).start())
    brecv[me_s] = bsend[me_s]
    each(STA, me_s, lambda peer: b_copy(peer, peer).wait_recv())
    each(STA, me_s, lambda peer: p_copy(peer, peer).wait_recv())

    left_lanes = lax.broadcasted_iota(jnp.int32, (WIN, ST), 1) < 64

    def one_pair(i, _):
        p = lax.rem(me_s + i, STA)
        a = pairs[p, 0, 0]
        b = pairs[p, 0, 1]
        a_odd = lax.rem(a, 2) == 1
        b_odd = lax.rem(b, 2) == 1
        first = brecv[a // 2]
        second = brecv[b // 2].astype(jnp.float32)
        for s in range(2):
            re, im = second[2 * s], second[2 * s + 1]
            re_roll, im_roll = pltpu.roll(re, 64, 1), pltpu.roll(im, 64, 1)
            re_l, im_l = jnp.where(b_odd, re_roll, re), jnp.where(b_odd, im_roll, im)
            re_r, im_r = jnp.where(b_odd, re, re_roll), jnp.where(b_odd, im, im_roll)
            right = jnp.concatenate(
                [jnp.where(left_lanes, re_l, -im_r), jnp.where(left_lanes, im_l, re_r)], axis=0
            ).astype(jnp.bfloat16)
            left = first[2 * s : 2 * s + 2].reshape(2 * WIN, ST)
            prod = lax.dot_general(left, right, (((0,), (0,)), ((), ())), preferred_element_type=jnp.float32)
            prod = jnp.where(a_odd, prod[64:], prod[:64])
            top, low = prod[:32], prod[32:]
            csend[p, 64 * s : 64 * s + 32, :] = jnp.where(left_lanes, top, pltpu.roll(low, 64, 1))
            csend[p, 64 * s + 32 : 64 * s + 64, :] = jnp.where(left_lanes, pltpu.roll(top, 64, 1), low)

        @pl.when(i < STA)
        def _():
            c_copy(p, me_s).start()

        return 0

    lax.fori_loop(1, STA + 1, one_pair, 0)
    crecv[me_s] = csend[me_s]
    each(STA, me_s, lambda peer: c_copy(peer, peer).wait_recv())

    for w in range(WIN):
        for z in range(STA):
            dsend[w, 4 * z : 4 * z + 4, :] = crecv[z, pl.ds(w, 4, stride=32), :]
    each(WIN, me_w, lambda peer: d_copy(peer, me_w).start())
    drecv[me_w] = dsend[me_w]
    t_copies[2].wait()
    each(WIN, me_w, lambda peer: d_copy(peer, peer).wait_recv())

    cross = drecv[...].reshape(WIN * 32, ST)
    high = cross.astype(jnp.bfloat16)
    low = (cross - high.astype(jnp.float32)).astype(jnp.bfloat16)
    both = jnp.concatenate([high, low], axis=1)

    def lags(t, _):
        row = pl.multiple_of(t * 128, 128)
        value = jnp.dot(lag_v[pl.ds(row, 128), :], both, preferred_element_type=jnp.float32)
        extra = jnp.dot(lag_v[pl.ds(row + LAGS, 128), :], high, preferred_element_type=jnp.float32)
        value = jnp.transpose(value[:, :ST] + (value[:, ST:] + extra))
        for i2 in range(2):
            for j2 in range(2):
                part = value[(2 * i2 + j2) * 32 : (2 * i2 + j2) * 32 + 32]
                order[pl.ds(i2 * 64 + j2, 32, stride=2), :] = part
        out_ref[:, :, pl.ds(row, 128)] = order[...].reshape(2, 64, 128)
        return 0

    lax.fori_loop(0, LAGS // 128, lags, 0)

    each(WIN, me_w, lambda peer: a_copy(peer, me_w).wait_send())
    each(STA, me_s, lambda peer: p_copy(peer, me_s).wait_send())
    each(STA, me_s, lambda peer: b_copy(peer, me_s).wait_send())
    each(STA, me_s, lambda peer: c_copy(peer, me_s).wait_send())
    each(WIN, me_w, lambda peer: d_copy(peer, me_w).wait_send())


def body(traces, pair_blocks):
    odd, even, lag = (jnp.asarray(t) for t in tables())
    f32, bf16 = jnp.float32, jnp.bfloat16
    hbm = pl.BlockSpec(memory_space=pl.ANY)
    out = pl.pallas_call(
        kernel,
        out_shape=jax.ShapeDtypeStruct((2, 64, LAGS), f32),
        in_specs=[hbm, pl.BlockSpec(memory_space=pltpu.SMEM), hbm, hbm, hbm],
        out_specs=pl.BlockSpec(memory_space=pltpu.VMEM),
        scratch_shapes=[
            pltpu.VMEM((ST * SEG, 128), f32),
            pltpu.VMEM(odd.shape, bf16),
            pltpu.VMEM(even.shape, bf16),
            pltpu.VMEM(lag.shape, bf16),
            pltpu.SMEM((STA, 1, 2), jnp.int32),
            pltpu.VMEM((7, 2 * ST, 2 * FOLD), bf16),
            pltpu.VMEM((2, 2 * ST, FOLD), bf16),
            pltpu.VMEM((2 * BANDS, ST), f32),
            pltpu.VMEM((WIN, 32, ST), bf16),
            pltpu.VMEM((WIN, 32, ST), bf16),
            pltpu.VMEM((STA, 4, WIN, ST), bf16),
            pltpu.VMEM((STA, 4, WIN, ST), bf16),
            pltpu.VMEM((STA, 128, ST), f32),
            pltpu.VMEM((STA, 128, ST), f32),
            pltpu.VMEM((WIN, 32, ST), f32),
            pltpu.VMEM((WIN, 32, ST), f32),
            pltpu.VMEM((ST, 128), f32),
            pltpu.SemaphoreType.DMA((4,)),
            pltpu.SemaphoreType.DMA((3,)),
        ]
        + [pltpu.SemaphoreType.DMA((n,)) for n in (STA, STA, WIN, WIN, STA, STA, STA, STA, WIN, WIN)],
        compiler_params=pltpu.CompilerParams(
            collective_id=0, has_side_effects=True, vmem_limit_bytes=48 * 1024 * 1024
        ),
        name="noise_correlation",
    )(traces.reshape(ST * SEG, 128), pair_blocks, odd, even, lag)
    return out.reshape(2, 1, 64, LAGS)


def solution(mesh):
    in_specs = (P("sta", "win", None), P("sta", None))
    out_specs = P("win", "sta", None, None)
    return jax.shard_map(body, mesh=mesh, in_specs=in_specs, out_specs=out_specs, check_vma=False)
```

```python
import functools
import math

import jax
import jax.numpy as jnp
import ml_dtypes
import numpy as np
from jax import lax
from jax.experimental import pallas as pl
from jax.experimental.pallas import tpu as pltpu
from jax.sharding import PartitionSpec as P

L = 8192
LAGS = 512
K0 = 256
BANDS = 512
STA = 8
WIN = 32
ST = 128
SEG = 64
RADIX = 16
FOLD = L // RADIX
MESH = pl.DeviceIdType.MESH


def bin_of():
    bins = np.zeros((WIN, STA, 2), np.int64)
    for z in range(STA):
        for q in range(1, 8):
            for u in range(4):
                m = 16 + 4 * z + u
                bins[4 * (q - 1) + u, z] = (16 * m + q, 16 * m + 16 - q)
        for half in range(2):
            for u in range(2):
                for s in range(2):
                    bins[28 + 2 * half + u, z, s] = 16 * (16 + 4 * z + 2 * u + s) + 8 * half
    return bins


def split(table):
    high = table.astype(ml_dtypes.bfloat16)
    low = (table - high.astype(np.float64)).astype(ml_dtypes.bfloat16)
    return high, low


@functools.cache
def tables():
    bins = bin_of()
    n = np.arange(FOLD)

    def trig(k):
        angle = 2 * math.pi * ((k * n) % L) / L
        return np.cos(angle), np.sin(angle)

    odd = np.zeros((7, 4, STA, 2, 2, 2 * FOLD))
    for q in range(1, 8):
        for u in range(4):
            for z in range(STA):
                for s in range(2):
                    c, d = trig(bins[4 * (q - 1) + u, z, s])
                    sign = 1.0 if s == 0 else -1.0
                    odd[q - 1, u, z, s, 0] = np.concatenate([c, sign * d])
                    odd[q - 1, u, z, s, 1] = np.concatenate([-d, sign * c])
    even = np.zeros((2, 2, STA, 2, 2, FOLD))
    for half in range(2):
        for u in range(2):
            for z in range(STA):
                for s in range(2):
                    c, d = trig(bins[28 + 2 * half + u, z, s])
                    even[half, u, z, s, 0] = c
                    even[half, u, z, s, 1] = -d
    shifts = (np.arange(LAGS) - LAGS // 2) % L
    angle = 2 * math.pi * ((bins[..., None] * shifts) % L) / L
    lag = np.stack([np.cos(angle), -np.sin(angle)], axis=3)
    lag = lag.transpose(2, 0, 1, 3, 4).reshape(2 * BANDS, LAGS).T * float(WIN * BANDS) ** (-0.5)
    odd = odd.transpose(0, 1, 3, 2, 4, 5).reshape(7, 128, 2 * FOLD)
    odd = np.stack(split(odd), axis=1)
    even = even.transpose(0, 1, 3, 2, 4, 5).reshape(2, 64, FOLD)
    even = np.stack(split(even), axis=1)
    lag = np.concatenate(split(lag), axis=0)
    return odd, even, lag


def fold16(x):
    r2 = math.sqrt(0.5)
    c1 = math.cos(math.pi / 8)
    c3 = math.sin(math.pi / 8)
    e = [x[a] + x[a + 8] for a in range(8)]
    o = [x[a] - x[a + 8] for a in range(8)]
    f = [e[a] + e[a + 4] for a in range(4)]
    g = [e[a] - e[a + 4] for a in range(4)]
    f02, f13 = f[0] + f[2], f[1] + f[3]
    gd, gs = r2 * (g[1] - g[3]), r2 * (g[1] + g[3])
    d = [None] + [o[a] - o[8 - a] for a in range(1, 4)]
    s = [None] + [o[a] + o[8 - a] for a in range(1, 4)]
    d2, s2 = r2 * d[2], r2 * s[2]
    p, m = o[0] + d2, o[0] - d2
    u, v = c1 * d[1] + c3 * d[3], c3 * d[1] - c1 * d[3]
    pp, mm = s2 + o[4], s2 - o[4]
    uu, vv = c3 * s[1] + c1 * s[3], c1 * s[1] - c3 * s[3]
    real = [f02 + f13, p + u, g[0] + gd, m + v, f[0] - f[2], m - v, g[0] - gd, p - u, f02 - f13]
    imag = [None, -(uu + pp), -(g[2] + gs), -(vv + mm), f[3] - f[1], mm - vv, g[2] - gs, pp - uu]
    return real, imag


def far_first_win():
    offsets = [(y, x, c) for y in range(4) for x in range(4) for c in range(2)][1:]
    return sorted(offsets, key=lambda o: -(10 * (min(o[0], 4 - o[0]) + min(o[1], 4 - o[1])) + o[2]))


FAR_FIRST_STA = (4, 3, 5, 2, 6, 1, 7)


def kernel(
    x_ref, pair_ref, odd_ref, even_ref, lag_ref, out_ref,
    x_v, odd_v, even_v, lag_v, pairs, fodd, feven, spec, rows, total, order,
    asend, arecv, bsend, brecv_0, brecv_1, csend, crecv, dsend, drecv,
    x_sem, t_sem, send_sem, p_sem, a_sem, b_sem, c_sem, d_sem,
):
    me_s = lax.axis_index("sta")
    me_w = lax.axis_index("win")
    y, x, core = me_w // 8, lax.rem(me_w // 2, 4), lax.rem(me_w, 2)
    ys = [lax.rem(y + d, 4) * 8 for d in range(4)]
    xs = [lax.rem(x + d, 4) * 2 for d in range(4)]
    cores = [core, 1 - core]
    win_peers = [ys[dy] + xs[dx] + cores[dc] for dy, dx, dc in far_first_win()]
    sta_peers = [lax.rem(me_s + d, STA) for d in FAR_FIRST_STA]

    x_copies = [
        pltpu.make_async_copy(x_ref.at[pl.ds(2048 * i, 2048)], x_v.at[pl.ds(2048 * i, 2048)], x_sem.at[i])
        for i in range(4)
    ]
    t_copies = [
        pltpu.make_async_copy(src, dst, t_sem.at[i])
        for i, (src, dst) in enumerate(((odd_ref, odd_v), (even_ref, even_v), (lag_ref, lag_v)))
    ]

    brecv = (brecv_0, brecv_1)
    barrier = pltpu.get_barrier_semaphore()
    for peer in win_peers:
        pl.semaphore_signal(barrier, inc=1, device_id={"win": peer}, device_id_type=MESH)
    for peer in sta_peers:
        pl.semaphore_signal(barrier, inc=1, device_id={"sta": peer}, device_id_type=MESH)
    for copy in x_copies + t_copies:
        copy.start()

    def send(src, dst, phase, recv_sem, axis, peer):
        pltpu.make_async_remote_copy(
            src_ref=src, dst_ref=dst, send_sem=send_sem.at[phase], recv_sem=recv_sem,
            device_id={axis: peer}, device_id_type=MESH,
        ).start()

    def wait(ref, sem):
        pltpu.make_async_copy(ref, ref, sem).wait()

    for chunk in range(4):
        x_copies[chunk].wait()

        def fold(t, _, chunk=chunk):
            lane_tile = lax.rem(t, 4)
            i2 = t // 4
            first = chunk * 2048 + i2 * 64
            x = [x_v[pl.ds(first + 4 * a + lane_tile, 16, stride=128), :] for a in range(RADIX)]
            real, imag = fold16(x)
            row = pl.multiple_of((chunk // 2) * 64 + i2 * 32 + (chunk % 2) * 16, 16)
            lane = pl.multiple_of(lane_tile * 128, 128)

            def put(dst, at, value):
                high = value.astype(jnp.bfloat16)
                low = (value - high.astype(jnp.float32)).astype(jnp.bfloat16)
                dst[pl.ds(row, 16), pl.ds(at, 128)] = high
                dst[pl.ds(row + 128, 16), pl.ds(at, 128)] = low

            put(feven.at[0], lane, real[0])
            put(feven.at[1], lane, real[8])
            for q in range(1, 8):
                put(fodd.at[q - 1], lane, real[q])
                put(fodd.at[q - 1], pl.multiple_of(lane + FOLD, 128), imag[q])
            return 0

        lax.fori_loop(0, 8, fold, 0)

    contract_last = (((1,), (1,)), ((), ()))

    def dft(table, data):
        high = lax.dot_general(table[0], data, contract_last, preferred_element_type=jnp.float32)
        low = lax.dot_general(table[1], data[:ST], contract_last, preferred_element_type=jnp.float32)
        return high[:, :ST] + (high[:, ST:] + low)

    t_copies[0].wait()

    def odd_class(q, power):
        value = dft(odd_v[q], fodd[q])
        spec[pl.ds(pl.multiple_of(q * 128, 128), 128), :] = value
        return power + jnp.sum((value * value).reshape(16, 8, ST), axis=0)

    power = lax.fori_loop(0, 7, odd_class, jnp.zeros((8, ST), jnp.float32))
    t_copies[1].wait()
    for half in range(2):
        value = dft(even_v[half], feven[half])
        spec[896 + 64 * half : 960 + 64 * half, :] = value
        power = power + jnp.sum((value * value).reshape(8, 8, ST), axis=0)
    mean = jnp.sum(power, axis=0, keepdims=True) * (1.0 / BANDS)
    inverse = 1.0 / jnp.sqrt(mean + 1e-06)
    for w in range(WIN):
        asend[w] = (spec[32 * w : 32 * w + 32, :] * inverse).astype(jnp.bfloat16).reshape(2, 16, ST)

    pl.semaphore_wait(barrier, STA - 1 + WIN - 1)

    for s in range(2):
        for peer in win_peers:
            send(asend.at[peer, s], arecv.at[s, me_w], 0, a_sem.at[s], "win", peer)
        arecv[s, me_w] = asend[me_w, s]
    for peer in sta_peers:
        send(pair_ref, pairs.at[me_s], 4, p_sem, "sta", peer)
    pairs[me_s, 0, 0] = pair_ref[0, 0]
    pairs[me_s, 0, 1] = pair_ref[0, 1]

    for s in range(2):
        wait(arecv.at[s, pl.ds(0, WIN - 1)], a_sem.at[s])
        rows[...] = arecv[s].reshape(WIN * 16, ST).astype(jnp.float32)
        for column in sta_peers + [me_s]:
            for c in range(2):
                part = rows[pl.ds(2 * column + c, WIN, stride=16), :].astype(jnp.bfloat16)
                bsend[column, s, WIN * c : WIN * c + WIN, :] = part
            if column is not me_s:
                send(bsend.at[column, s], brecv[s].at[me_s], 1, b_sem.at[s], "sta", column)
        brecv[s][me_s] = bsend[me_s, s]

    left_lanes = lax.broadcasted_iota(jnp.int32, (WIN, ST), 1) < 64

    def cross(p, s):
        a = pairs[p, 0, 0]
        b = pairs[p, 0, 1]
        a_odd = lax.rem(a, 2) == 1
        b_odd = lax.rem(b, 2) == 1
        left = brecv[s][a // 2]
        second = brecv[s][b // 2].astype(jnp.float32)
        re, im = second[:WIN], second[WIN:]
        re_roll, im_roll = pltpu.roll(re, 64, 1), pltpu.roll(im, 64, 1)
        re_l, im_l = jnp.where(b_odd, re_roll, re), jnp.where(b_odd, im_roll, im)
        re_r, im_r = jnp.where(b_odd, re, re_roll), jnp.where(b_odd, im, im_roll)
        right = jnp.concatenate(
            [jnp.where(left_lanes, re_l, -im_r), jnp.where(left_lanes, im_l, re_r)], axis=0
        ).astype(jnp.bfloat16)
        prod = lax.dot_general(left, right, (((0,), (0,)), ((), ())), preferred_element_type=jnp.float32)
        prod = jnp.where(a_odd, prod[64:], prod[:64])
        top, low = prod[:32], prod[32:]
        value = jnp.concatenate(
            [jnp.where(left_lanes, top, pltpu.roll(low, 64, 1)), jnp.where(left_lanes, pltpu.roll(top, 64, 1), low)],
            axis=0,
        ).reshape(8, 8, ST)
        largest = jnp.maximum(jnp.max(jnp.abs(value), axis=0), 1e-30)
        exponent = jnp.floor(jnp.log(largest) * (1.0 / math.log(2.0))) + 1.0
        scaled = jnp.round(value * jnp.exp2(15.0 - exponent)[None])
        scaled = jnp.clip(scaled, -32767.0, 32767.0).reshape(64, ST)
        csend[p, s, :64, :] = scaled.astype(jnp.int32).astype(jnp.int16)
        csend[p, s, 64:, :] = jnp.concatenate([exponent, exponent], axis=0).astype(jnp.int32).astype(jnp.int16)

    for s in range(2):
        wait(brecv[s].at[pl.ds(0, STA - 1)], b_sem.at[s])
        if s == 0:
            wait(pairs.at[pl.ds(0, STA - 1)], p_sem)
        for p in sta_peers:
            cross(p, s)
            send(csend.at[p, s], crecv.at[me_s, s], 2, c_sem.at[s], "sta", p)
        cross(me_s, s)
        crecv[me_s, s] = csend[me_s, s]

    for s in range(2):
        wait(crecv.at[pl.ds(0, STA - 1), s], c_sem.at[s])
        for z in range(STA):
            scale = jnp.exp2(crecv[z, s, 64:, :].astype(jnp.float32)[:8] - 15.0)
            value = crecv[z, s, :64, :].astype(jnp.float32).reshape(8, 8, ST) * scale[None]
            rows[64 * z : 64 * z + 64, :] = value.reshape(64, ST)
        for w in win_peers + [me_w]:
            dsend[w, s] = rows[pl.ds(w, 16, stride=32), :]
            if w is not me_w:
                send(dsend.at[w, s], drecv.at[s, me_w], 3, d_sem.at[s], "win", w)
        drecv[s, me_w] = dsend[me_w, s]

    t_copies[2].wait()
    wait(asend.at[pl.ds(0, WIN - 1)], send_sem.at[0])
    wait(bsend.at[pl.ds(0, STA - 1)], send_sem.at[1])
    wait(csend.at[pl.ds(0, STA - 1)], send_sem.at[2])
    wait(pairs.at[pl.ds(0, STA - 1)], send_sem.at[4])

    for s in range(2):
        wait(drecv.at[s, pl.ds(0, WIN - 1)], d_sem.at[s])
        value = drecv[s].reshape(BANDS, ST)
        high = value.astype(jnp.bfloat16)
        low = (value - high.astype(jnp.float32)).astype(jnp.bfloat16)
        both = jnp.concatenate([high, low], axis=1)

        def lags(t, _, s=s, both=both, high=high):
            row = pl.multiple_of(t * 128, 128)
            lane = pl.multiple_of(s * BANDS, 128)
            value = jnp.dot(
                lag_v[pl.ds(row, 128), pl.ds(lane, BANDS)], both, preferred_element_type=jnp.float32
            )
            extra = jnp.dot(
                lag_v[pl.ds(row + LAGS, 128), pl.ds(lane, BANDS)], high, preferred_element_type=jnp.float32
            )
            value = value[:, :ST] + (value[:, ST:] + extra)
            if s == 0:
                total[pl.ds(row, 128), :] = value
                return 0
            value = jnp.transpose(value + total[pl.ds(row, 128), :])
            for i2 in range(2):
                for j2 in range(2):
                    part = value[(2 * i2 + j2) * 32 : (2 * i2 + j2) * 32 + 32]
                    order[pl.ds(i2 * 64 + j2, 32, stride=2), :] = part
            out_ref[:, :, pl.ds(row, 128)] = order[...].reshape(2, 64, 128)
            return 0

        lax.fori_loop(0, LAGS // 128, lags, 0)
    wait(dsend.at[pl.ds(0, WIN - 1)], send_sem.at[3])


def body(traces, pair_blocks):
    odd, even, lag = (jnp.asarray(t) for t in tables())
    f32, bf16, i16 = jnp.float32, jnp.bfloat16, jnp.int16
    hbm = pl.BlockSpec(memory_space=pltpu.HBM)
    out = pl.pallas_call(
        kernel,
        out_shape=jax.ShapeDtypeStruct((2, 64, LAGS), f32),
        in_specs=[hbm, pl.BlockSpec(memory_space=pltpu.SMEM), hbm, hbm, hbm],
        out_specs=pl.BlockSpec(memory_space=pltpu.VMEM),
        scratch_shapes=[
            pltpu.VMEM((ST * SEG, 128), f32),
            pltpu.VMEM(odd.shape, bf16),
            pltpu.VMEM(even.shape, bf16),
            pltpu.VMEM(lag.shape, bf16),
            pltpu.SMEM((STA, 1, 2), jnp.int32),
            pltpu.VMEM((7, 2 * ST, 2 * FOLD), bf16),
            pltpu.VMEM((2, 2 * ST, FOLD), bf16),
            pltpu.VMEM((2 * BANDS, ST), f32),
            pltpu.VMEM((BANDS, ST), f32),
            pltpu.VMEM((LAGS, ST), f32),
            pltpu.VMEM((ST, 128), f32),
            pltpu.VMEM((WIN, 2, 16, ST), bf16),
            pltpu.VMEM((2, WIN, 16, ST), bf16),
            pltpu.VMEM((STA, 2, 2 * WIN, ST), bf16),
            pltpu.VMEM((STA, 2 * WIN, ST), bf16),
            pltpu.VMEM((STA, 2 * WIN, ST), bf16),
            pltpu.VMEM((STA, 2, 80, ST), i16),
            pltpu.VMEM((STA, 2, 80, ST), i16),
            pltpu.VMEM((WIN, 2, 16, ST), f32),
            pltpu.VMEM((2, WIN, 16, ST), f32),
            pltpu.SemaphoreType.DMA((4,)),
            pltpu.SemaphoreType.DMA((3,)),
            pltpu.SemaphoreType.DMA((5,)),
            pltpu.SemaphoreType.DMA,
            pltpu.SemaphoreType.DMA((2,)),
            pltpu.SemaphoreType.DMA((2,)),
            pltpu.SemaphoreType.DMA((2,)),
            pltpu.SemaphoreType.DMA((2,)),
        ],
        compiler_params=pltpu.CompilerParams(
            collective_id=0, has_side_effects=True, vmem_limit_bytes=48 * 1024 * 1024
        ),
        name="noise_correlation",
    )(traces.reshape(ST * SEG, 128), pair_blocks, odd, even, lag)
    return out.reshape(2, 1, 64, LAGS)


def solution(mesh):
    in_specs = (P("sta", "win", None), P("sta", None))
    out_specs = P("win", "sta", None, None)
    return jax.shard_map(body, mesh=mesh, in_specs=in_specs, out_specs=out_specs, check_vma=False)
```

```python
import functools
import math

import jax
import jax.numpy as jnp
import ml_dtypes
import numpy as np
from jax import lax
from jax.experimental import pallas as pl
from jax.experimental.pallas import tpu as pltpu
from jax.sharding import PartitionSpec as P

L = 8192
LAGS = 512
K0 = 256
BANDS = 512
STA = 8
WIN = 32
ST = 128
SEG = 64
RADIX = 16
FOLD = L // RADIX
MESH = pl.DeviceIdType.MESH


def bin_of():
    bins = np.zeros((WIN, STA, 2), np.int64)
    for z in range(STA):
        for q in range(1, 8):
            for u in range(4):
                m = 16 + 4 * z + u
                bins[4 * (q - 1) + u, z] = (16 * m + q, 16 * m + 16 - q)
        for half in range(2):
            for u in range(2):
                for s in range(2):
                    bins[28 + 2 * half + u, z, s] = 16 * (16 + 4 * z + 2 * u + s) + 8 * half
    return bins


def split(table):
    high = table.astype(ml_dtypes.bfloat16)
    low = (table - high.astype(np.float64)).astype(ml_dtypes.bfloat16)
    return high, low


@functools.cache
def tables():
    bins = bin_of()
    n = np.arange(FOLD)

    def trig(k):
        angle = 2 * math.pi * ((k * n) % L) / L
        return np.cos(angle), np.sin(angle)

    odd = np.zeros((7, 4, STA, 2, 2, 2 * FOLD))
    for q in range(1, 8):
        for u in range(4):
            for z in range(STA):
                for s in range(2):
                    c, d = trig(bins[4 * (q - 1) + u, z, s])
                    sign = 1.0 if s == 0 else -1.0
                    odd[q - 1, u, z, s, 0] = np.concatenate([c, sign * d])
                    odd[q - 1, u, z, s, 1] = np.concatenate([-d, sign * c])
    even = np.zeros((2, 2, STA, 2, 2, FOLD))
    for half in range(2):
        for u in range(2):
            for z in range(STA):
                for s in range(2):
                    c, d = trig(bins[28 + 2 * half + u, z, s])
                    even[half, u, z, s, 0] = c
                    even[half, u, z, s, 1] = -d
    shifts = (np.arange(LAGS) - LAGS // 2) % L
    angle = 2 * math.pi * ((bins[..., None] * shifts) % L) / L
    lag = np.stack([np.cos(angle), -np.sin(angle)], axis=3)
    lag = lag.transpose(2, 3, 1, 0, 4).reshape(2 * BANDS, LAGS).T * float(WIN * BANDS) ** (-0.5)
    odd = np.stack(split(odd.reshape(7, 128, 2 * FOLD)), axis=1)
    even = np.stack(split(even.reshape(2, 64, FOLD)), axis=1)
    lag = np.concatenate(split(lag), axis=0)
    return odd, even, lag


def fold16(x):
    r2 = math.sqrt(0.5)
    c1 = math.cos(math.pi / 8)
    c3 = math.sin(math.pi / 8)
    e = [x[a] + x[a + 8] for a in range(8)]
    o = [x[a] - x[a + 8] for a in range(8)]
    f = [e[a] + e[a + 4] for a in range(4)]
    g = [e[a] - e[a + 4] for a in range(4)]
    f02, f13 = f[0] + f[2], f[1] + f[3]
    gd, gs = r2 * (g[1] - g[3]), r2 * (g[1] + g[3])
    d = [None] + [o[a] - o[8 - a] for a in range(1, 4)]
    s = [None] + [o[a] + o[8 - a] for a in range(1, 4)]
    d2, s2 = r2 * d[2], r2 * s[2]
    p, m = o[0] + d2, o[0] - d2
    u, v = c1 * d[1] + c3 * d[3], c3 * d[1] - c1 * d[3]
    pp, mm = s2 + o[4], s2 - o[4]
    uu, vv = c3 * s[1] + c1 * s[3], c1 * s[1] - c3 * s[3]
    real = [f02 + f13, p + u, g[0] + gd, m + v, f[0] - f[2], m - v, g[0] - gd, p - u, f02 - f13]
    imag = [None, -(uu + pp), -(g[2] + gs), -(vv + mm), f[3] - f[1], mm - vv, g[2] - gs, pp - uu]
    return real, imag


FAR_FIRST = ((4,), (3, 5), (2, 6), (1, 7), (0,))
ALL = STA * WIN


def kernel(
    x_ref, pair_ref, odd_ref, even_ref, lag_ref, out_ref,
    x_v, odd_v, even_v, lag_v, pairs, fodd, feven, spec, rows, codes, order,
    asend, arecv, bands, csend, crecv,
    x_sem, t_sem, send_sem, p_sem, a_sem, c_sem,
):
    me_s = lax.axis_index("sta")
    me_w = lax.axis_index("win")
    me = me_s * WIN + me_w

    x_copies = [
        pltpu.make_async_copy(x_ref.at[pl.ds(2048 * i, 2048)], x_v.at[pl.ds(2048 * i, 2048)], x_sem.at[i])
        for i in range(4)
    ]
    t_copies = [
        pltpu.make_async_copy(src, dst, t_sem.at[i])
        for i, (src, dst) in enumerate(((odd_ref, odd_v), (even_ref, even_v), (lag_ref, lag_v)))
    ]
    for copy in x_copies + t_copies:
        copy.start()

    def column(offset):
        return lax.rem(me_s + offset, STA)

    def to_others(action):
        def in_columns(offsets):
            def step(i, _):
                w = lax.rem(me_w + (1 if 0 in offsets else 20) + i, WIN)
                for offset in offsets:
                    action(column(offset), w)
                return 0

            lax.fori_loop(0, WIN - 1 if 0 in offsets else WIN, step, 0)

        for offsets in FAR_FIRST:
            in_columns(offsets)

    barrier = pltpu.get_barrier_semaphore()

    def greet(z, w):
        pl.semaphore_signal(barrier, inc=1, device_id={"sta": z, "win": w}, device_id_type=MESH)

    to_others(greet)

    def send(src, dst, phase, recv_sem, z, w):
        pltpu.make_async_remote_copy(
            src_ref=src, dst_ref=dst, send_sem=send_sem.at[phase], recv_sem=recv_sem,
            device_id={"sta": z, "win": w}, device_id_type=MESH,
        ).start()

    def wait(ref, sem):
        pltpu.make_async_copy(ref, ref, sem).wait()

    for chunk in range(4):
        x_copies[chunk].wait()

        def fold(t, _, chunk=chunk):
            lane_tile = lax.rem(t, 4)
            i2 = t // 4
            first = chunk * 2048 + i2 * 64
            x = [x_v[pl.ds(first + 4 * a + lane_tile, 16, stride=128), :] for a in range(RADIX)]
            real, imag = fold16(x)
            row = pl.multiple_of((chunk // 2) * 64 + i2 * 32 + (chunk % 2) * 16, 16)
            lane = pl.multiple_of(lane_tile * 128, 128)

            def put(dst, at, value):
                high = value.astype(jnp.bfloat16)
                low = (value - high.astype(jnp.float32)).astype(jnp.bfloat16)
                dst[pl.ds(row, 16), pl.ds(at, 128)] = high
                dst[pl.ds(row + 128, 16), pl.ds(at, 128)] = low

            put(feven.at[0], lane, real[0])
            put(feven.at[1], lane, real[8])
            for q in range(1, 8):
                put(fodd.at[q - 1], lane, real[q])
                put(fodd.at[q - 1], pl.multiple_of(lane + FOLD, 128), imag[q])
            return 0

        lax.fori_loop(0, 8, fold, 0)

    contract_last = (((1,), (1,)), ((), ()))

    def dft(table, data):
        high = lax.dot_general(table[0], data, contract_last, preferred_element_type=jnp.float32)
        low = lax.dot_general(table[1], data[:ST], contract_last, preferred_element_type=jnp.float32)
        return high[:, :ST] + (high[:, ST:] + low)

    t_copies[0].wait()

    def odd_class(q, power):
        value = dft(odd_v[q], fodd[q])
        spec[pl.ds(pl.multiple_of(q * 128, 128), 128), :] = value
        return power + jnp.sum((value * value).reshape(16, 8, ST), axis=0)

    power = lax.fori_loop(0, 7, odd_class, jnp.zeros((8, ST), jnp.float32))
    t_copies[1].wait()
    for half in range(2):
        value = dft(even_v[half], feven[half])
        spec[896 + 64 * half : 960 + 64 * half, :] = value
        power = power + jnp.sum((value * value).reshape(8, 8, ST), axis=0)
    mean = jnp.sum(power, axis=0, keepdims=True) * (1.0 / BANDS)
    inverse = 1.0 / jnp.sqrt(mean + 1e-06)
    for i in range(ALL // 8):
        white = (spec[32 * i : 32 * i + 32, :] * inverse).astype(jnp.bfloat16)
        asend[8 * i : 8 * i + 8] = white.reshape(8, 4, ST)

    pl.semaphore_wait(barrier, ALL - 1)

    to_others(lambda z, w: send(asend.at[w * STA + z], arecv.at[me], 0, a_sem, z, w))
    for offsets in FAR_FIRST[:-1]:
        for offset in offsets:
            send(pair_ref, pairs.at[me_s], 2, p_sem, column(offset), me_w)
    arecv[me] = asend[me_w * STA + me_s]
    pairs[me_s, 0, 0] = pair_ref[0, 0]
    pairs[me_s, 0, 1] = pair_ref[0, 1]
    wait(arecv.at[pl.ds(0, ALL - 1)], a_sem)

    for z in range(STA):
        part = arecv[WIN * z : WIN * z + WIN].astype(jnp.float32)
        rows[128 * z : 128 * z + 128, :] = part.reshape(4 * WIN, ST)
    for z in range(STA):
        for r in range(4):
            part = rows[pl.ds(128 * z + r, WIN, stride=4), :]
            bands[z, WIN * r : WIN * r + WIN, :] = part.astype(jnp.bfloat16)
    wait(pairs.at[pl.ds(0, STA - 1)], p_sem)

    left_lanes = lax.broadcasted_iota(jnp.int32, (WIN, ST), 1) < 64

    def cross(p):
        a = pairs[p, 0, 0]
        b = pairs[p, 0, 1]
        a_odd = lax.rem(a, 2) == 1
        b_odd = lax.rem(b, 2) == 1
        first = bands[a // 2]
        second = bands[b // 2].astype(jnp.float32)
        parts = []
        for s in range(2):
            re, im = second[64 * s : 64 * s + 32], second[64 * s + 32 : 64 * s + 64]
            re_roll, im_roll = pltpu.roll(re, 64, 1), pltpu.roll(im, 64, 1)
            re_l, im_l = jnp.where(b_odd, re_roll, re), jnp.where(b_odd, im_roll, im)
            re_r, im_r = jnp.where(b_odd, re, re_roll), jnp.where(b_odd, im, im_roll)
            right = jnp.concatenate(
                [jnp.where(left_lanes, re_l, -im_r), jnp.where(left_lanes, im_l, re_r)], axis=0
            ).astype(jnp.bfloat16)
            left = first[64 * s : 64 * s + 64]
            prod = lax.dot_general(left, right, (((0,), (0,)), ((), ())), preferred_element_type=jnp.float32)
            prod = jnp.where(a_odd, prod[64:], prod[:64])
            top, low = prod[:32], prod[32:]
            parts.append(jnp.where(left_lanes, top, pltpu.roll(low, 64, 1)))
            parts.append(jnp.where(left_lanes, pltpu.roll(top, 64, 1), low))
        return parts

    def encode(p, parts):
        largest = functools.reduce(jnp.maximum, [jnp.abs(v) for v in parts])
        exponent = jnp.floor(jnp.log(jnp.maximum(largest, 1e-30)) * (1.0 / math.log(2.0))) + 1.0
        scale = jnp.exp2(13.0 - exponent)
        exponent = exponent.astype(jnp.int32) + 128
        for r, v in enumerate(parts):
            value = jnp.clip(jnp.round(v * scale), -8191.0, 8191.0).astype(jnp.int32)
            codes[pl.ds(r, WIN, stride=4), :] = value * 4 + (jnp.right_shift(exponent, 2 * r) & 3)
        csend[pl.ds(WIN * p, WIN)] = codes[:128, :].astype(jnp.int16).reshape(WIN, 4, ST)

    for offsets in FAR_FIRST:
        for offset in offsets:
            p = column(offset)
            encode(p, cross(p))

            def step(i, _, p=p, offset=offset):
                w = lax.rem(me_w + (20 if offset else 1) + i, WIN)
                send(csend.at[p * WIN + w], crecv.at[me], 1, c_sem, p, w)
                return 0

            lax.fori_loop(0, WIN if offset else WIN - 1, step, 0)
    crecv[me] = csend[me]

    t_copies[2].wait()
    wait(asend.at[pl.ds(0, ALL - 1)], send_sem.at[0])
    wait(pairs.at[pl.ds(0, STA - 1)], send_sem.at[2])
    wait(crecv.at[pl.ds(0, ALL - 1)], c_sem)

    for z in range(STA):
        part = crecv[WIN * z : WIN * z + WIN].astype(jnp.int32)
        codes[128 * z : 128 * z + 128, :] = part.reshape(4 * WIN, ST)
    coded = [codes[pl.ds(r, ALL, stride=4), :] for r in range(4)]
    exponent = functools.reduce(jnp.bitwise_or, [jnp.left_shift(v & 3, 2 * r) for r, v in enumerate(coded)])
    scale = jnp.exp2((exponent - 141).astype(jnp.float32))
    value = jnp.concatenate([jnp.right_shift(v, 2).astype(jnp.float32) * scale for v in coded], axis=0)
    high = value.astype(jnp.bfloat16)
    low = (value - high.astype(jnp.float32)).astype(jnp.bfloat16)
    both = jnp.concatenate([high, low], axis=1)

    def lags(t, _):
        row = pl.multiple_of(t * 128, 128)
        value = jnp.dot(lag_v[pl.ds(row, 128), :], both, preferred_element_type=jnp.float32)
        extra = jnp.dot(lag_v[pl.ds(row + LAGS, 128), :], high, preferred_element_type=jnp.float32)
        value = jnp.transpose(value[:, :ST] + (value[:, ST:] + extra))
        for i2 in range(2):
            for j2 in range(2):
                part = value[(2 * i2 + j2) * 32 : (2 * i2 + j2) * 32 + 32]
                order[pl.ds(i2 * 64 + j2, 32, stride=2), :] = part
        out_ref[:, :, pl.ds(row, 128)] = order[...].reshape(2, 64, 128)
        return 0

    lax.fori_loop(0, LAGS // 128, lags, 0)
    wait(csend.at[pl.ds(0, ALL - 1)], send_sem.at[1])


def body(traces, pair_blocks):
    odd, even, lag = (jnp.asarray(t) for t in tables())
    f32, bf16, i16 = jnp.float32, jnp.bfloat16, jnp.int16
    hbm = pl.BlockSpec(memory_space=pltpu.HBM)
    out = pl.pallas_call(
        kernel,
        out_shape=jax.ShapeDtypeStruct((2, 64, LAGS), f32),
        in_specs=[hbm, pl.BlockSpec(memory_space=pltpu.SMEM), hbm, hbm, hbm],
        out_specs=pl.BlockSpec(memory_space=pltpu.VMEM),
        scratch_shapes=[
            pltpu.VMEM((ST * SEG, 128), f32),
            pltpu.VMEM(odd.shape, bf16),
            pltpu.VMEM(even.shape, bf16),
            pltpu.VMEM(lag.shape, bf16),
            pltpu.SMEM((STA, 1, 2), jnp.int32),
            pltpu.VMEM((7, 2 * ST, 2 * FOLD), bf16),
            pltpu.VMEM((2, 2 * ST, FOLD), bf16),
            pltpu.VMEM((2 * BANDS, ST), f32),
            pltpu.VMEM((2 * BANDS, ST), f32),
            pltpu.VMEM((2 * BANDS, ST), jnp.int32),
            pltpu.VMEM((ST, 128), f32),
            pltpu.VMEM((ALL, 4, ST), bf16),
            pltpu.VMEM((ALL, 4, ST), bf16),
            pltpu.VMEM((STA, 4 * WIN, ST), bf16),
            pltpu.VMEM((ALL, 4, ST), i16),
            pltpu.VMEM((ALL, 4, ST), i16),
            pltpu.SemaphoreType.DMA((4,)),
            pltpu.SemaphoreType.DMA((3,)),
            pltpu.SemaphoreType.DMA((3,)),
            pltpu.SemaphoreType.DMA,
            pltpu.SemaphoreType.DMA,
            pltpu.SemaphoreType.DMA,
        ],
        compiler_params=pltpu.CompilerParams(
            collective_id=0, has_side_effects=True, vmem_limit_bytes=48 * 1024 * 1024
        ),
        name="noise_correlation",
    )(traces.reshape(ST * SEG, 128), pair_blocks, odd, even, lag)
    return out.reshape(2, 1, 64, LAGS)


def solution(mesh):
    in_specs = (P("sta", "win", None), P("sta", None))
    out_specs = P("win", "sta", None, None)
    return jax.shard_map(body, mesh=mesh, in_specs=in_specs, out_specs=out_specs, check_vma=False)
```

```python
import functools
import math

import jax
import jax.numpy as jnp
import ml_dtypes
import numpy as np
from jax import lax
from jax.experimental import pallas as pl
from jax.experimental.pallas import tpu as pltpu
from jax.sharding import PartitionSpec as P

L = 8192
LAGS = 512
K0 = 256
BANDS = 512
STA = 8
WIN = 32
ST = 128
SEG = 64
RADIX = 16
FOLD = L // RADIX
ODD = 7 * 2 * FOLD
MESH = pl.DeviceIdType.MESH


def bin_of():
    bins = np.zeros((WIN, STA, 2), np.int64)
    for z in range(STA):
        for q in range(1, 8):
            for u in range(4):
                m = 16 + 4 * z + u
                bins[4 * (q - 1) + u, z] = (16 * m + q, 16 * m + 16 - q)
        for half in range(2):
            for u in range(2):
                for s in range(2):
                    bins[28 + 2 * half + u, z, s] = 16 * (16 + 4 * z + 2 * u + s) + 8 * half
    return bins


def split(table):
    high = table.astype(ml_dtypes.bfloat16)
    low = (table - high.astype(np.float64)).astype(ml_dtypes.bfloat16)
    return high, low


@functools.cache
def tables():
    bins = bin_of()
    n = np.arange(FOLD)

    def trig(k):
        angle = 2 * math.pi * ((k * n) % L) / L
        return np.cos(angle), np.sin(angle)

    odd = np.zeros((7, 4, STA, 2, 2, 2 * FOLD))
    for q in range(1, 8):
        for u in range(4):
            for z in range(STA):
                for s in range(2):
                    c, d = trig(bins[4 * (q - 1) + u, z, s])
                    sign = 1.0 if s == 0 else -1.0
                    odd[q - 1, u, z, s, 0] = np.concatenate([c, sign * d])
                    odd[q - 1, u, z, s, 1] = np.concatenate([-d, sign * c])
    even = np.zeros((2, 2, STA, 2, 2, FOLD))
    for half in range(2):
        for u in range(2):
            for z in range(STA):
                for s in range(2):
                    c, d = trig(bins[28 + 2 * half + u, z, s])
                    even[half, u, z, s, 0] = c
                    even[half, u, z, s, 1] = -d
    shifts = (np.arange(LAGS) - LAGS // 2) % L
    angle = 2 * math.pi * ((bins[..., None] * shifts) % L) / L
    lag = np.stack([np.cos(angle), -np.sin(angle)], axis=3)
    lag = lag.transpose(2, 3, 1, 0, 4).reshape(2 * BANDS, LAGS).T * float(WIN * BANDS) ** (-0.5)
    odd = np.concatenate(split(odd.reshape(7, 128, 2 * FOLD).transpose(0, 2, 1)), axis=2).reshape(ODD, 256)
    even = np.concatenate(split(even.reshape(2, 64, FOLD).transpose(0, 2, 1)), axis=2)
    even = even.transpose(1, 0, 2).reshape(FOLD, 256)
    lag = np.concatenate(split(lag), axis=0).reshape(2 * LAGS, 4, 256).transpose(1, 0, 2).reshape(8 * LAGS, 256)
    return np.concatenate([odd, even, lag], axis=0)


def fold16(x):
    r2 = math.sqrt(0.5)
    c1 = math.cos(math.pi / 8)
    c3 = math.sin(math.pi / 8)
    e = [x[a] + x[a + 8] for a in range(8)]
    o = [x[a] - x[a + 8] for a in range(8)]
    f = [e[a] + e[a + 4] for a in range(4)]
    g = [e[a] - e[a + 4] for a in range(4)]
    f02, f13 = f[0] + f[2], f[1] + f[3]
    gd, gs = r2 * (g[1] - g[3]), r2 * (g[1] + g[3])
    d = [None] + [o[a] - o[8 - a] for a in range(1, 4)]
    s = [None] + [o[a] + o[8 - a] for a in range(1, 4)]
    d2, s2 = r2 * d[2], r2 * s[2]
    p, m = o[0] + d2, o[0] - d2
    u, v = c1 * d[1] + c3 * d[3], c3 * d[1] - c1 * d[3]
    pp, mm = s2 + o[4], s2 - o[4]
    uu, vv = c3 * s[1] + c1 * s[3], c1 * s[1] - c3 * s[3]
    real = [f02 + f13, p + u, g[0] + gd, m + v, f[0] - f[2], m - v, g[0] - gd, p - u, f02 - f13]
    imag = [None, -(uu + pp), -(g[2] + gs), -(vv + mm), f[3] - f[1], mm - vv, g[2] - gs, pp - uu]
    return real, imag


FAR_FIRST = ((4,), (3, 5), (2, 6), (1, 7), (0,))
ALL = STA * WIN


def kernel(
    x_ref, pair_ref, table_ref, out_ref,
    x_v, odd_v, even_v, lag_v, pairs, fodd, feven, spec, rows, codes, order,
    asend, arecv, bands, csend, crecv,
    x_sem, t_sem, send_sem, p_sem, a_sem, c_sem, ready_sem,
):
    me_s = lax.axis_index("sta")
    me_w = lax.axis_index("win")
    me = me_s * WIN + me_w

    x_copies = [
        pltpu.make_async_copy(x_ref.at[pl.ds(2048 * i, 2048)], x_v.at[pl.ds(2048 * i, 2048)], x_sem.at[i])
        for i in range(4)
    ]
    pieces = [(odd_v.at[pl.ds(1024 * q, 1024)], 1024 * q) for q in range(7)]
    pieces += [(even_v, ODD), (lag_v, ODD + FOLD)]
    t_copies = [
        pltpu.make_async_copy(table_ref.at[pl.ds(first, dst.shape[0])], dst, t_sem.at[i])
        for i, (dst, first) in enumerate(pieces)
    ]
    for copy in x_copies + t_copies:
        copy.start()

    def column(offset):
        return lax.rem(me_s + offset, STA)

    def to_others(action):
        def in_columns(offsets):
            def step(i, _):
                w = lax.rem(me_w + (1 if 0 in offsets else 20) + i, WIN)
                for offset in offsets:
                    action(column(offset), w)
                return 0

            lax.fori_loop(0, WIN - 1 if 0 in offsets else WIN, step, 0)

        for offsets in FAR_FIRST:
            in_columns(offsets)

    barrier = pltpu.get_barrier_semaphore()

    def to_columns(action):
        for offsets in FAR_FIRST[:-1]:
            for offset in offsets:
                action(column(offset))

    def greet(i, _):
        peer = lax.rem(me_w + i, WIN)
        pl.semaphore_signal(barrier, inc=1, device_id={"win": peer}, device_id_type=MESH)
        return 0

    lax.fori_loop(1, WIN, greet, 0)
    to_columns(lambda z: pl.semaphore_signal(barrier, inc=1, device_id={"sta": z}, device_id_type=MESH))

    def send(src, dst, phase, recv_sem, z, w):
        pltpu.make_async_remote_copy(
            src_ref=src, dst_ref=dst, send_sem=send_sem.at[phase], recv_sem=recv_sem,
            device_id={"sta": z, "win": w}, device_id_type=MESH,
        ).start()

    def wait(ref, sem):
        pltpu.make_async_copy(ref, ref, sem).wait()

    for chunk in range(4):
        x_copies[chunk].wait()

        def fold(t, _, chunk=chunk):
            lane_tile = lax.rem(t, 4)
            i2 = t // 4
            first = chunk * 2048 + i2 * 64
            x = [x_v[pl.ds(first + 4 * a + lane_tile, 16, stride=128), :] for a in range(RADIX)]
            real, imag = fold16(x)
            row = pl.multiple_of((chunk // 2) * 64 + i2 * 32 + (chunk % 2) * 16, 16)
            lane = pl.multiple_of(lane_tile * 128, 128)

            def put(dst, at, value):
                high = value.astype(jnp.bfloat16)
                low = (value - high.astype(jnp.float32)).astype(jnp.bfloat16)
                dst[pl.ds(row, 16), pl.ds(at, 128)] = high
                dst[pl.ds(row + 128, 16), pl.ds(at, 128)] = low

            put(feven.at[0], lane, real[0])
            put(feven.at[1], lane, real[8])
            for q in range(1, 8):
                put(fodd.at[q - 1], lane, real[q])
                put(fodd.at[q - 1], pl.multiple_of(lane + FOLD, 128), imag[q])
            return 0

        lax.fori_loop(0, 8, fold, 0)

    pl.semaphore_wait(barrier, STA - 1 + WIN - 1)
    to_columns(lambda z: pl.semaphore_signal(ready_sem, inc=1, device_id={"sta": z}, device_id_type=MESH))

    def dft(data, table):
        prod = jnp.dot(data, table, preferred_element_type=jnp.float32)
        bins = prod.shape[1] // 2
        return jnp.transpose(prod[:ST, :bins] + (prod[:ST, bins:] + prod[ST:, :bins]))

    power = jnp.zeros((8, ST), jnp.float32)
    for q in range(7):
        t_copies[q].wait()
        value = dft(fodd[q], odd_v[1024 * q : 1024 * q + 1024])
        spec[128 * q : 128 * q + 128, :] = value
        power = power + jnp.sum((value * value).reshape(16, 8, ST), axis=0)
    t_copies[7].wait()
    for half in range(2):
        value = dft(feven[half], even_v[:, 128 * half : 128 * half + 128])
        spec[896 + 64 * half : 960 + 64 * half, :] = value
        power = power + jnp.sum((value * value).reshape(8, 8, ST), axis=0)
    mean = jnp.sum(power, axis=0, keepdims=True) * (1.0 / BANDS)
    inverse = 1.0 / jnp.sqrt(mean + 1e-06)
    for i in range(ALL // 8):
        white = (spec[32 * i : 32 * i + 32, :] * inverse).astype(jnp.bfloat16)
        asend[8 * i : 8 * i + 8] = white.reshape(8, 4, ST)

    pl.semaphore_wait(ready_sem, STA - 1)

    to_others(lambda z, w: send(asend.at[w * STA + z], arecv.at[me], 0, a_sem, z, w))
    to_columns(lambda z: send(pair_ref, pairs.at[me_s], 2, p_sem, z, me_w))
    arecv[me] = asend[me_w * STA + me_s]
    pairs[me_s, 0, 0] = pair_ref[0, 0]
    pairs[me_s, 0, 1] = pair_ref[0, 1]
    wait(arecv.at[pl.ds(0, ALL - 1)], a_sem)

    for z in range(STA):
        part = arecv[WIN * z : WIN * z + WIN].astype(jnp.float32)
        rows[128 * z : 128 * z + 128, :] = part.reshape(4 * WIN, ST)
    for z in range(STA):
        for r in range(4):
            part = rows[pl.ds(128 * z + r, WIN, stride=4), :]
            bands[z, WIN * r : WIN * r + WIN, :] = part.astype(jnp.bfloat16)
    wait(pairs.at[pl.ds(0, STA - 1)], p_sem)

    left_lanes = lax.broadcasted_iota(jnp.int32, (WIN, ST), 1) < 64

    def cross(p):
        a = pairs[p, 0, 0]
        b = pairs[p, 0, 1]
        a_odd = lax.rem(a, 2) == 1
        b_odd = lax.rem(b, 2) == 1
        first = bands[a // 2]
        second = bands[b // 2].astype(jnp.float32)
        parts = []
        for s in range(2):
            re, im = second[64 * s : 64 * s + 32], second[64 * s + 32 : 64 * s + 64]
            re_roll, im_roll = pltpu.roll(re, 64, 1), pltpu.roll(im, 64, 1)
            re_l, im_l = jnp.where(b_odd, re_roll, re), jnp.where(b_odd, im_roll, im)
            re_r, im_r = jnp.where(b_odd, re, re_roll), jnp.where(b_odd, im, im_roll)
            right = jnp.concatenate(
                [jnp.where(left_lanes, re_l, -im_r), jnp.where(left_lanes, im_l, re_r)], axis=0
            ).astype(jnp.bfloat16)
            left = first[64 * s : 64 * s + 64]
            prod = lax.dot_general(left, right, (((0,), (0,)), ((), ())), preferred_element_type=jnp.float32)
            prod = jnp.where(a_odd, prod[64:], prod[:64])
            top, low = prod[:32], prod[32:]
            parts.append(jnp.where(left_lanes, top, pltpu.roll(low, 64, 1)))
            parts.append(jnp.where(left_lanes, pltpu.roll(top, 64, 1), low))
        return parts

    def encode(p, parts):
        largest = functools.reduce(jnp.maximum, [jnp.abs(v) for v in parts])
        exponent = jnp.floor(jnp.log(jnp.maximum(largest, 1e-30)) * (1.0 / math.log(2.0))) + 1.0
        scale = jnp.exp2(13.0 - exponent)
        exponent = exponent.astype(jnp.int32) + 128
        for r, v in enumerate(parts):
            value = jnp.clip(jnp.round(v * scale), -8191.0, 8191.0).astype(jnp.int32)
            codes[pl.ds(r, WIN, stride=4), :] = value * 4 + (jnp.right_shift(exponent, 2 * r) & 3)
        csend[pl.ds(WIN * p, WIN)] = codes[:128, :].astype(jnp.int16).reshape(WIN, 4, ST)

    for offsets in FAR_FIRST:
        for offset in offsets:
            p = column(offset)
            encode(p, cross(p))

            def step(i, _, p=p, offset=offset):
                w = lax.rem(me_w + (20 if offset else 1) + i, WIN)
                send(csend.at[p * WIN + w], crecv.at[me], 1, c_sem, p, w)
                return 0

            lax.fori_loop(0, WIN if offset else WIN - 1, step, 0)
    crecv[me] = csend[me]

    t_copies[8].wait()
    wait(asend.at[pl.ds(0, ALL - 1)], send_sem.at[0])
    wait(pairs.at[pl.ds(0, STA - 1)], send_sem.at[2])
    wait(crecv.at[pl.ds(0, ALL - 1)], c_sem)

    for z in range(STA):
        part = crecv[WIN * z : WIN * z + WIN].astype(jnp.int32)
        codes[128 * z : 128 * z + 128, :] = part.reshape(4 * WIN, ST)
    coded = [codes[pl.ds(r, ALL, stride=4), :] for r in range(4)]
    exponent = functools.reduce(jnp.bitwise_or, [jnp.left_shift(v & 3, 2 * r) for r, v in enumerate(coded)])
    scale = jnp.exp2((exponent - 141).astype(jnp.float32))
    value = jnp.concatenate([jnp.right_shift(v, 2).astype(jnp.float32) * scale for v in coded], axis=0)
    high = value.astype(jnp.bfloat16)
    low = (value - high.astype(jnp.float32)).astype(jnp.bfloat16)
    both = jnp.concatenate([high, low], axis=1)

    def lags(t, _):
        row = pl.multiple_of(t * 128, 128)
        value = jnp.zeros((128, 2 * ST), jnp.float32)
        extra = jnp.zeros((128, ST), jnp.float32)
        for block in range(4):
            first = 2 * LAGS * block
            part = both[256 * block : 256 * block + 256]
            value += jnp.dot(lag_v[pl.ds(first + row, 128), :], part, preferred_element_type=jnp.float32)
            extra += jnp.dot(
                lag_v[pl.ds(first + LAGS + row, 128), :], part[:, :ST], preferred_element_type=jnp.float32
            )
        value = jnp.transpose(value[:, :ST] + (value[:, ST:] + extra))
        for i2 in range(2):
            for j2 in range(2):
                part = value[(2 * i2 + j2) * 32 : (2 * i2 + j2) * 32 + 32]
                order[pl.ds(i2 * 64 + j2, 32, stride=2), :] = part
        out_ref[:, :, pl.ds(row, 128)] = order[...].reshape(2, 64, 128)
        return 0

    lax.fori_loop(0, LAGS // 128, lags, 0)
    wait(csend.at[pl.ds(0, ALL - 1)], send_sem.at[1])


def body(traces, pair_blocks):
    table = jnp.asarray(tables())
    f32, bf16, i16 = jnp.float32, jnp.bfloat16, jnp.int16
    hbm = pl.BlockSpec(memory_space=pltpu.HBM)
    out = pl.pallas_call(
        kernel,
        out_shape=jax.ShapeDtypeStruct((2, 64, LAGS), f32),
        in_specs=[hbm, pl.BlockSpec(memory_space=pltpu.SMEM), hbm],
        out_specs=pl.BlockSpec(memory_space=pltpu.VMEM),
        scratch_shapes=[
            pltpu.VMEM((ST * SEG, 128), f32),
            pltpu.VMEM((ODD, 256), bf16),
            pltpu.VMEM((FOLD, 256), bf16),
            pltpu.VMEM((8 * LAGS, 256), bf16),
            pltpu.SMEM((STA, 1, 2), jnp.int32),
            pltpu.VMEM((7, 2 * ST, 2 * FOLD), bf16),
            pltpu.VMEM((2, 2 * ST, FOLD), bf16),
            pltpu.VMEM((2 * BANDS, ST), f32),
            pltpu.VMEM((2 * BANDS, ST), f32),
            pltpu.VMEM((2 * BANDS, ST), jnp.int32),
            pltpu.VMEM((ST, 128), f32),
            pltpu.VMEM((ALL, 4, ST), bf16),
            pltpu.VMEM((ALL, 4, ST), bf16),
            pltpu.VMEM((STA, 4 * WIN, ST), bf16),
            pltpu.VMEM((ALL, 4, ST), i16),
            pltpu.VMEM((ALL, 4, ST), i16),
            pltpu.SemaphoreType.DMA((4,)),
            pltpu.SemaphoreType.DMA((9,)),
            pltpu.SemaphoreType.DMA((3,)),
            pltpu.SemaphoreType.DMA,
            pltpu.SemaphoreType.DMA,
            pltpu.SemaphoreType.DMA,
            pltpu.SemaphoreType.REGULAR,
        ],
        compiler_params=pltpu.CompilerParams(
            collective_id=0, has_side_effects=True, vmem_limit_bytes=58 * 1024 * 1024
        ),
        name="noise_correlation",
    )(traces.reshape(ST * SEG, 128), pair_blocks, table)
    return out.reshape(2, 1, 64, LAGS)


def solution(mesh):
    in_specs = (P("sta", "win", None), P("sta", None))
    out_specs = P("win", "sta", None, None)
    return jax.shard_map(body, mesh=mesh, in_specs=in_specs, out_specs=out_specs, check_vma=False)
```

```python
import functools
import math

import jax
import jax.numpy as jnp
import ml_dtypes
import numpy as np
from jax import lax
from jax.experimental import pallas as pl
from jax.experimental.pallas import tpu as pltpu
from jax.sharding import PartitionSpec as P

L = 8192
LAGS = 512
K0 = 256
BANDS = 512
STA = 8
WIN = 32
ST = 128
SEG = 64
RADIX = 16
FOLD = L // RADIX
ODD = 7 * 2 * FOLD
MESH = pl.DeviceIdType.MESH


def bin_of():
    bins = np.zeros((WIN, STA, 2), np.int64)
    for z in range(STA):
        for q in range(1, 8):
            for u in range(4):
                m = 16 + 4 * z + u
                bins[4 * (q - 1) + u, z] = (16 * m + q, 16 * m + 16 - q)
        for half in range(2):
            for u in range(2):
                for s in range(2):
                    bins[28 + 2 * half + u, z, s] = 16 * (16 + 4 * z + 2 * u + s) + 8 * half
    return bins


def split(table):
    high = table.astype(ml_dtypes.bfloat16)
    low = (table - high.astype(np.float64)).astype(ml_dtypes.bfloat16)
    return high, low


@functools.cache
def tables():
    bins = bin_of()
    n = np.arange(FOLD)

    def trig(k):
        angle = 2 * math.pi * ((k * n) % L) / L
        return np.cos(angle), np.sin(angle)

    odd = np.zeros((7, 4, STA, 2, 2, 2 * FOLD))
    for q in range(1, 8):
        for u in range(4):
            for z in range(STA):
                for s in range(2):
                    c, d = trig(bins[4 * (q - 1) + u, z, s])
                    sign = 1.0 if s == 0 else -1.0
                    odd[q - 1, u, z, s, 0] = np.concatenate([c, sign * d])
                    odd[q - 1, u, z, s, 1] = np.concatenate([-d, sign * c])
    even = np.zeros((2, 2, STA, 2, 2, FOLD))
    for half in range(2):
        for u in range(2):
            for z in range(STA):
                for s in range(2):
                    c, d = trig(bins[28 + 2 * half + u, z, s])
                    even[half, u, z, s, 0] = c
                    even[half, u, z, s, 1] = -d
    shifts = (np.arange(LAGS) - LAGS // 2) % L
    angle = 2 * math.pi * ((bins[..., None] * shifts) % L) / L
    lag = np.stack([np.cos(angle), -np.sin(angle)], axis=3)
    lag = lag.transpose(2, 3, 1, 0, 4).reshape(2 * BANDS, LAGS).T * float(WIN * BANDS) ** (-0.5)
    odd = np.concatenate(split(odd.reshape(7, 128, 2 * FOLD).transpose(0, 2, 1)), axis=2).reshape(ODD, 256)
    even = np.concatenate(split(even.reshape(128, FOLD).T), axis=1)
    lag = np.concatenate(split(lag), axis=0).reshape(2 * LAGS, 4, 256).transpose(1, 0, 2).reshape(8 * LAGS, 256)
    return np.concatenate([odd, even, lag], axis=0)


def fold16(x):
    r2 = math.sqrt(0.5)
    c1 = math.cos(math.pi / 8)
    c3 = math.sin(math.pi / 8)
    e = [x[a] + x[a + 8] for a in range(8)]
    o = [x[a] - x[a + 8] for a in range(8)]
    f = [e[a] + e[a + 4] for a in range(4)]
    g = [e[a] - e[a + 4] for a in range(4)]
    f02, f13 = f[0] + f[2], f[1] + f[3]
    gd, gs = r2 * (g[1] - g[3]), r2 * (g[1] + g[3])
    d = [None] + [o[a] - o[8 - a] for a in range(1, 4)]
    s = [None] + [o[a] + o[8 - a] for a in range(1, 4)]
    d2, s2 = r2 * d[2], r2 * s[2]
    p, m = o[0] + d2, o[0] - d2
    u, v = c1 * d[1] + c3 * d[3], c3 * d[1] - c1 * d[3]
    pp, mm = s2 + o[4], s2 - o[4]
    uu, vv = c3 * s[1] + c1 * s[3], c1 * s[1] - c3 * s[3]
    real = [f02 + f13, p + u, g[0] + gd, m + v, f[0] - f[2], m - v, g[0] - gd, p - u, f02 - f13]
    imag = [None, -(uu + pp), -(g[2] + gs), -(vv + mm), f[3] - f[1], mm - vv, g[2] - gs, pp - uu]
    return real, imag


FAR_FIRST = ((4,), (3, 5), (2, 6), (1, 7), (0,))
ALL = STA * WIN


def kernel(
    x_ref, pair_ref, table_ref, out_ref,
    x_v, odd_v, even_v, lag_v, pairs, fodd, feven, spec, rows, codes, order,
    asend, arecv, bands, csend, crecv,
    x_sem, t_sem, send_sem, p_sem, a_sem, c_sem,
):
    me_s = lax.axis_index("sta")
    me_w = lax.axis_index("win")
    me = me_s * WIN + me_w

    x_copies = [
        pltpu.make_async_copy(x_ref.at[pl.ds(2048 * i, 2048)], x_v.at[pl.ds(2048 * i, 2048)], x_sem.at[i])
        for i in range(4)
    ]
    t_copies = [
        pltpu.make_async_copy(table_ref.at[pl.ds(first, dst.shape[0])], dst, t_sem.at[i])
        for i, (first, dst) in enumerate(((0, odd_v), (ODD, even_v), (ODD + FOLD, lag_v)))
    ]
    for copy in x_copies + t_copies:
        copy.start()

    def column(offset):
        return lax.rem(me_s + offset, STA)

    def to_others(action):
        def in_columns(offsets):
            def step(i, _):
                w = lax.rem(me_w + (1 if 0 in offsets else 20) + i, WIN)
                for offset in offsets:
                    action(column(offset), w)
                return 0

            lax.fori_loop(0, WIN - 1 if 0 in offsets else WIN, step, 0)

        for offsets in FAR_FIRST:
            in_columns(offsets)

    barrier = pltpu.get_barrier_semaphore()

    def greet(offset, i):
        w = lax.rem(me_w + i, WIN)
        pl.semaphore_signal(barrier, inc=1, device_id={"sta": column(offset), "win": w}, device_id_type=MESH)

    def greet_early(i, _):
        for offset in (4, 3, 5):
            greet(offset, i)
        return 0

    lax.fori_loop(0, WIN, greet_early, 0)

    def send(src, dst, phase, recv_sem, z, w):
        pltpu.make_async_remote_copy(
            src_ref=src, dst_ref=dst, send_sem=send_sem.at[phase], recv_sem=recv_sem,
            device_id={"sta": z, "win": w}, device_id_type=MESH,
        ).start()

    def wait(ref, sem):
        pltpu.make_async_copy(ref, ref, sem).wait()

    for chunk in range(4):
        x_copies[chunk].wait()

        def fold(t, _, chunk=chunk):
            if chunk < 2:
                for offset in (2, 6, 1, 7, 0):
                    for i in range(2):
                        greet(offset, 16 * chunk + 2 * t + i)
            lane_tile = lax.rem(t, 4)
            i2 = t // 4
            first = chunk * 2048 + i2 * 64
            x = [x_v[pl.ds(first + 4 * a + lane_tile, 16, stride=128), :] for a in range(RADIX)]
            real, imag = fold16(x)
            row = pl.multiple_of((chunk // 2) * 64 + i2 * 32 + (chunk % 2) * 16, 16)
            lane = pl.multiple_of(lane_tile * 128, 128)

            def put(dst, at, value):
                high = value.astype(jnp.bfloat16)
                low = (value - high.astype(jnp.float32)).astype(jnp.bfloat16)
                dst[pl.ds(row, 16), pl.ds(at, 128)] = high
                dst[pl.ds(row + 128, 16), pl.ds(at, 128)] = low

            put(feven.at[0], lane, real[0])
            put(feven.at[1], lane, real[8])
            for q in range(1, 8):
                put(fodd.at[q - 1], lane, real[q])
                put(fodd.at[q - 1], pl.multiple_of(lane + FOLD, 128), imag[q])
            return 0

        lax.fori_loop(0, 8, fold, 0)

    def dft(data, table):
        prod = jnp.dot(data, table, preferred_element_type=jnp.float32)
        return prod[:ST, :128] + (prod[:ST, 128:] + prod[ST:, :128])

    t_copies[0].wait()
    t_copies[1].wait()
    power = jnp.zeros((8, ST), jnp.float32)
    for q in range(8):
        if q < 7:
            value = dft(fodd[q], odd_v[1024 * q : 1024 * q + 1024])
        else:
            first_half = lax.broadcasted_iota(jnp.int32, (ST, 128), 1) < 64
            value = jnp.where(first_half, dft(feven[0], even_v[...]), dft(feven[1], even_v[...]))
        value = jnp.transpose(value)
        spec[128 * q : 128 * q + 128, :] = value
        power = power + jnp.sum((value * value).reshape(16, 8, ST), axis=0)
    mean = jnp.sum(power, axis=0, keepdims=True) * (1.0 / BANDS)
    inverse = 1.0 / jnp.sqrt(mean + 1e-06)
    for i in range(ALL // 8):
        white = (spec[32 * i : 32 * i + 32, :] * inverse).astype(jnp.bfloat16)
        asend[8 * i : 8 * i + 8] = white.reshape(8, 4, ST)

    pl.semaphore_wait(barrier, ALL)

    to_others(lambda z, w: send(asend.at[w * STA + z], arecv.at[me], 0, a_sem, z, w))
    for offset in range(1, STA):
        send(pair_ref, pairs.at[me_s], 2, p_sem, column(offset), me_w)
    arecv[me] = asend[me_w * STA + me_s]
    pairs[me_s, 0, 0] = pair_ref[0, 0]
    pairs[me_s, 0, 1] = pair_ref[0, 1]
    wait(arecv.at[pl.ds(0, ALL - 1)], a_sem)

    for z in range(STA):
        part = arecv[WIN * z : WIN * z + WIN].astype(jnp.float32)
        rows[128 * z : 128 * z + 128, :] = part.reshape(4 * WIN, ST)
    for z in range(STA):
        for r in range(4):
            part = rows[pl.ds(128 * z + r, WIN, stride=4), :]
            bands[z, WIN * r : WIN * r + WIN, :] = part.astype(jnp.bfloat16)
    wait(pairs.at[pl.ds(0, STA - 1)], p_sem)

    left_lanes = lax.broadcasted_iota(jnp.int32, (WIN, ST), 1) < 64

    def cross(p):
        a = pairs[p, 0, 0]
        b = pairs[p, 0, 1]
        a_odd = lax.rem(a, 2) == 1
        b_odd = lax.rem(b, 2) == 1
        first = bands[a // 2]
        second = bands[b // 2].astype(jnp.float32)
        parts = []
        for s in range(2):
            re, im = second[64 * s : 64 * s + 32], second[64 * s + 32 : 64 * s + 64]
            re_roll, im_roll = pltpu.roll(re, 64, 1), pltpu.roll(im, 64, 1)
            re_l, im_l = jnp.where(b_odd, re_roll, re), jnp.where(b_odd, im_roll, im)
            re_r, im_r = jnp.where(b_odd, re, re_roll), jnp.where(b_odd, im, im_roll)
            right = jnp.concatenate(
                [jnp.where(left_lanes, re_l, -im_r), jnp.where(left_lanes, im_l, re_r)], axis=0
            ).astype(jnp.bfloat16)
            left = first[64 * s : 64 * s + 64]
            prod = lax.dot_general(left, right, (((0,), (0,)), ((), ())), preferred_element_type=jnp.float32)
            prod = jnp.where(a_odd, prod[64:], prod[:64])
            top, low = prod[:32], prod[32:]
            parts.append(jnp.where(left_lanes, top, pltpu.roll(low, 64, 1)))
            parts.append(jnp.where(left_lanes, pltpu.roll(top, 64, 1), low))
        return parts

    def encode(p, parts):
        largest = functools.reduce(jnp.maximum, [jnp.abs(v) for v in parts])
        exponent = jnp.floor(jnp.log(jnp.maximum(largest, 1e-30)) * (1.0 / math.log(2.0))) + 1.0
        scale = jnp.exp2(13.0 - exponent)
        exponent = exponent.astype(jnp.int32) + 128
        for r, v in enumerate(parts):
            value = jnp.clip(jnp.round(v * scale), -8191.0, 8191.0).astype(jnp.int32)
            codes[pl.ds(r, WIN, stride=4), :] = value * 4 + (jnp.right_shift(exponent, 2 * r) & 3)
        csend[pl.ds(WIN * p, WIN)] = codes[:128, :].astype(jnp.int16).reshape(WIN, 4, ST)

    for offsets in FAR_FIRST:
        for offset in offsets:
            p = column(offset)
            encode(p, cross(p))

            def step(i, _, p=p, offset=offset):
                w = lax.rem(me_w + (20 if offset else 1) + i, WIN)
                send(csend.at[p * WIN + w], crecv.at[me], 1, c_sem, p, w)
                return 0

            lax.fori_loop(0, WIN if offset else WIN - 1, step, 0)
    crecv[me] = csend[me]

    t_copies[2].wait()
    wait(asend.at[pl.ds(0, ALL - 1)], send_sem.at[0])
    wait(pairs.at[pl.ds(0, STA - 1)], send_sem.at[2])
    wait(crecv.at[pl.ds(0, ALL - 1)], c_sem)

    for z in range(STA):
        part = crecv[WIN * z : WIN * z + WIN].astype(jnp.int32)
        codes[128 * z : 128 * z + 128, :] = part.reshape(4 * WIN, ST)
    coded = [codes[pl.ds(r, ALL, stride=4), :] for r in range(4)]
    exponent = functools.reduce(jnp.bitwise_or, [jnp.left_shift(v & 3, 2 * r) for r, v in enumerate(coded)])
    scale = jnp.exp2((exponent - 141).astype(jnp.float32))
    value = jnp.concatenate([jnp.right_shift(v, 2).astype(jnp.float32) * scale for v in coded], axis=0)
    high = value.astype(jnp.bfloat16)
    low = (value - high.astype(jnp.float32)).astype(jnp.bfloat16)
    both = jnp.concatenate([high, low], axis=1)

    def lags(t, _):
        row = pl.multiple_of(t * 128, 128)
        value = jnp.zeros((128, 2 * ST), jnp.float32)
        extra = jnp.zeros((128, ST), jnp.float32)
        for block in range(4):
            first = 2 * LAGS * block
            part = both[256 * block : 256 * block + 256]
            value += jnp.dot(lag_v[pl.ds(first + row, 128), :], part, preferred_element_type=jnp.float32)
            extra += jnp.dot(
                lag_v[pl.ds(first + LAGS + row, 128), :], part[:, :ST], preferred_element_type=jnp.float32
            )
        value = jnp.transpose(value[:, :ST] + (value[:, ST:] + extra))
        for i2 in range(2):
            for j2 in range(2):
                part = value[(2 * i2 + j2) * 32 : (2 * i2 + j2) * 32 + 32]
                order[pl.ds(i2 * 64 + j2, 32, stride=2), :] = part
        out_ref[:, :, pl.ds(row, 128)] = order[...].reshape(2, 64, 128)
        return 0

    lax.fori_loop(0, LAGS // 128, lags, 0)
    wait(csend.at[pl.ds(0, ALL - 1)], send_sem.at[1])


def body(traces, pair_blocks):
    table = jnp.asarray(tables())
    f32, bf16, i16 = jnp.float32, jnp.bfloat16, jnp.int16
    hbm = pl.BlockSpec(memory_space=pltpu.HBM)
    out = pl.pallas_call(
        kernel,
        out_shape=jax.ShapeDtypeStruct((2, 64, LAGS), f32),
        in_specs=[hbm, pl.BlockSpec(memory_space=pltpu.SMEM), hbm],
        out_specs=pl.BlockSpec(memory_space=pltpu.VMEM),
        scratch_shapes=[
            pltpu.VMEM((ST * SEG, 128), f32),
            pltpu.VMEM((ODD, 256), bf16),
            pltpu.VMEM((FOLD, 256), bf16),
            pltpu.VMEM((8 * LAGS, 256), bf16),
            pltpu.SMEM((STA, 1, 2), jnp.int32),
            pltpu.VMEM((7, 2 * ST, 2 * FOLD), bf16),
            pltpu.VMEM((2, 2 * ST, FOLD), bf16),
            pltpu.VMEM((2 * BANDS, ST), f32),
            pltpu.VMEM((2 * BANDS, ST), f32),
            pltpu.VMEM((2 * BANDS, ST), jnp.int32),
            pltpu.VMEM((ST, 128), f32),
            pltpu.VMEM((ALL, 4, ST), bf16),
            pltpu.VMEM((ALL, 4, ST), bf16),
            pltpu.VMEM((STA, 4 * WIN, ST), bf16),
            pltpu.VMEM((ALL, 4, ST), i16),
            pltpu.VMEM((ALL, 4, ST), i16),
            pltpu.SemaphoreType.DMA((4,)),
            pltpu.SemaphoreType.DMA((3,)),
            pltpu.SemaphoreType.DMA((3,)),
            pltpu.SemaphoreType.DMA,
            pltpu.SemaphoreType.DMA,
            pltpu.SemaphoreType.DMA,
        ],
        compiler_params=pltpu.CompilerParams(
            collective_id=0, has_side_effects=True, vmem_limit_bytes=58 * 1024 * 1024
        ),
        name="noise_correlation",
    )(traces.reshape(ST * SEG, 128), pair_blocks, table)
    return out.reshape(2, 1, 64, LAGS)


def solution(mesh):
    in_specs = (P("sta", "win", None), P("sta", None))
    out_specs = P("win", "sta", None, None)
    return jax.shard_map(body, mesh=mesh, in_specs=in_specs, out_specs=out_specs, check_vma=False)
```

```python
import functools
import math

import jax
import jax.numpy as jnp
import ml_dtypes
import numpy as np
from jax import lax
from jax.experimental import pallas as pl
from jax.experimental.pallas import tpu as pltpu
from jax.sharding import PartitionSpec as P

L = 8192
LAGS = 512
K0 = 256
BANDS = 512
STA = 8
WIN = 32
ST = 128
SEG = 64
RADIX = 16
FOLD = L // RADIX
ODD = 7 * 2 * FOLD
MESH = pl.DeviceIdType.MESH


def bin_of():
    bins = np.zeros((WIN, STA, 2), np.int64)
    for z in range(STA):
        for q in range(1, 8):
            for u in range(4):
                m = 16 + 4 * z + u
                bins[4 * (q - 1) + u, z] = (16 * m + q, 16 * m + 16 - q)
        for half in range(2):
            for u in range(2):
                for s in range(2):
                    bins[28 + 2 * half + u, z, s] = 16 * (16 + 4 * z + 2 * u + s) + 8 * half
    return bins


def split(table):
    high = table.astype(ml_dtypes.bfloat16)
    low = (table - high.astype(np.float64)).astype(ml_dtypes.bfloat16)
    return high, low


@functools.cache
def tables():
    bins = bin_of()
    n = np.arange(FOLD)

    def trig(k):
        angle = 2 * math.pi * ((k * n) % L) / L
        return np.cos(angle), np.sin(angle)

    odd = np.zeros((7, 4, STA, 2, 2, 2 * FOLD))
    for q in range(1, 8):
        for u in range(4):
            for z in range(STA):
                for s in range(2):
                    c, d = trig(bins[4 * (q - 1) + u, z, s])
                    sign = 1.0 if s == 0 else -1.0
                    odd[q - 1, u, z, s, 0] = np.concatenate([c, sign * d])
                    odd[q - 1, u, z, s, 1] = np.concatenate([-d, sign * c])
    even = np.zeros((2, 2, STA, 2, 2, FOLD))
    for half in range(2):
        for u in range(2):
            for z in range(STA):
                for s in range(2):
                    c, d = trig(bins[28 + 2 * half + u, z, s])
                    even[half, u, z, s, 0] = c
                    even[half, u, z, s, 1] = -d
    shifts = (np.arange(LAGS) - LAGS // 2) % L
    angle = 2 * math.pi * ((bins[..., None] * shifts) % L) / L
    lag = np.stack([np.cos(angle), -np.sin(angle)], axis=3)
    lag = lag.transpose(2, 3, 1, 0, 4).reshape(2 * BANDS, LAGS).T * float(WIN * BANDS) ** (-0.5)
    odd = np.concatenate(split(odd.transpose(0, 3, 1, 2, 4, 5).reshape(7, 128, 2 * FOLD).transpose(0, 2, 1)), axis=2).reshape(ODD, 256)
    even = np.concatenate(split(even.transpose(3, 0, 1, 2, 4, 5).reshape(128, FOLD).T), axis=1)
    lag = np.concatenate(split(lag), axis=0).reshape(2 * LAGS, 4, 256).transpose(1, 0, 2).reshape(8 * LAGS, 256)
    return np.concatenate([odd, even, lag], axis=0)


def fold16(x):
    r2 = math.sqrt(0.5)
    c1 = math.cos(math.pi / 8)
    c3 = math.sin(math.pi / 8)
    e = [x[a] + x[a + 8] for a in range(8)]
    o = [x[a] - x[a + 8] for a in range(8)]
    f = [e[a] + e[a + 4] for a in range(4)]
    g = [e[a] - e[a + 4] for a in range(4)]
    f02, f13 = f[0] + f[2], f[1] + f[3]
    gd, gs = r2 * (g[1] - g[3]), r2 * (g[1] + g[3])
    d = [None] + [o[a] - o[8 - a] for a in range(1, 4)]
    s = [None] + [o[a] + o[8 - a] for a in range(1, 4)]
    d2, s2 = r2 * d[2], r2 * s[2]
    p, m = o[0] + d2, o[0] - d2
    u, v = c1 * d[1] + c3 * d[3], c3 * d[1] - c1 * d[3]
    pp, mm = s2 + o[4], s2 - o[4]
    uu, vv = c3 * s[1] + c1 * s[3], c1 * s[1] - c3 * s[3]
    real = [f02 + f13, p + u, g[0] + gd, m + v, f[0] - f[2], m - v, g[0] - gd, p - u, f02 - f13]
    imag = [None, -(uu + pp), -(g[2] + gs), -(vv + mm), f[3] - f[1], mm - vv, g[2] - gs, pp - uu]
    return real, imag


FAR_FIRST = ((4,), (3, 5), (2, 6), (1, 7), (0,))
ALL = STA * WIN


def kernel(
    x_ref, pair_ref, table_ref, out_ref,
    x_v, odd_v, even_v, lag_v, pairs, fodd, feven, spec, rows, bands, codes, total, order,
    asend_0, asend_1, arecv_0, arecv_1, csend_0, csend_1, crecv_0, crecv_1,
    x_sem, t_sem, send_sem, p_sem, a_sem, c_sem,
):
    me_s = lax.axis_index("sta")
    me_w = lax.axis_index("win")
    me = me_s * WIN + me_w
    asend, arecv = (asend_0, asend_1), (arecv_0, arecv_1)
    csend, crecv = (csend_0, csend_1), (crecv_0, crecv_1)

    x_copies = [
        pltpu.make_async_copy(x_ref.at[pl.ds(2048 * i, 2048)], x_v.at[pl.ds(2048 * i, 2048)], x_sem.at[i])
        for i in range(4)
    ]
    t_copies = [
        pltpu.make_async_copy(table_ref.at[pl.ds(first, dst.shape[0])], dst, t_sem.at[i])
        for i, (first, dst) in enumerate(((0, odd_v), (ODD, even_v), (ODD + FOLD, lag_v)))
    ]
    for copy in x_copies + t_copies[:2]:
        copy.start()

    def column(offset):
        return lax.rem(me_s + offset, STA)

    def to_others(action):
        def in_columns(offsets):
            def step(i, _):
                w = lax.rem(me_w + (1 if 0 in offsets else 20) + i, WIN)
                for offset in offsets:
                    action(column(offset), w)
                return 0

            lax.fori_loop(0, WIN - 1 if 0 in offsets else WIN, step, 0)

        for offsets in FAR_FIRST:
            in_columns(offsets)

    barrier = pltpu.get_barrier_semaphore()

    def greet(offset, i):
        w = lax.rem(me_w + i, WIN)
        pl.semaphore_signal(barrier, inc=1, device_id={"sta": column(offset), "win": w}, device_id_type=MESH)

    def greet_early(i, _):
        for offset in (4, 3, 5):
            greet(offset, i)
        return 0

    lax.fori_loop(0, WIN, greet_early, 0)

    def send(src, dst, phase, recv_sem, z, w):
        pltpu.make_async_remote_copy(
            src_ref=src, dst_ref=dst, send_sem=send_sem.at[phase], recv_sem=recv_sem,
            device_id={"sta": z, "win": w}, device_id_type=MESH,
        ).start()

    def wait(ref, sem):
        pltpu.make_async_copy(ref, ref, sem).wait()

    for chunk in range(4):
        x_copies[chunk].wait()

        def fold(t, _, chunk=chunk):
            if chunk < 2:
                for offset in (2, 6, 1, 7, 0):
                    for i in range(2):
                        greet(offset, 16 * chunk + 2 * t + i)
            lane_tile = lax.rem(t, 4)
            i2 = t // 4
            first = chunk * 2048 + i2 * 64
            x = [x_v[pl.ds(first + 4 * a + lane_tile, 16, stride=128), :] for a in range(RADIX)]
            real, imag = fold16(x)
            row = pl.multiple_of((chunk // 2) * 64 + i2 * 32 + (chunk % 2) * 16, 16)
            lane = pl.multiple_of(lane_tile * 128, 128)

            def put(dst, at, value):
                high = value.astype(jnp.bfloat16)
                low = (value - high.astype(jnp.float32)).astype(jnp.bfloat16)
                dst[pl.ds(row, 16), pl.ds(at, 128)] = high
                dst[pl.ds(row + 128, 16), pl.ds(at, 128)] = low

            put(feven.at[0], lane, real[0])
            put(feven.at[1], lane, real[8])
            for q in range(1, 8):
                put(fodd.at[q - 1], lane, real[q])
                put(fodd.at[q - 1], pl.multiple_of(lane + FOLD, 128), imag[q])
            return 0

        lax.fori_loop(0, 8, fold, 0)

    def dft(data, table):
        prod = jnp.dot(data, table, preferred_element_type=jnp.float32)
        return prod[:ST, :128] + (prod[:ST, 128:] + prod[ST:, :128])

    t_copies[0].wait()
    t_copies[1].wait()
    t_copies[2].start()
    power = jnp.zeros((8, ST), jnp.float32)
    for q in range(8):
        if q < 7:
            value = dft(fodd[q], odd_v[1024 * q : 1024 * q + 1024])
        else:
            first_half = lax.rem(lax.broadcasted_iota(jnp.int32, (ST, 128), 1), 64) < 32
            value = jnp.where(first_half, dft(feven[0], even_v[...]), dft(feven[1], even_v[...]))
        value = jnp.transpose(value)
        spec[128 * q : 128 * q + 128, :] = value
        power = power + jnp.sum((value * value).reshape(16, 8, ST), axis=0)
    mean = jnp.sum(power, axis=0, keepdims=True) * (1.0 / BANDS)
    inverse = 1.0 / jnp.sqrt(mean + 1e-06)
    for q in range(8):
        for s in range(2):
            first = 128 * q + 64 * s
            white = (spec[first : first + 64, :] * inverse).astype(jnp.bfloat16)
            asend[s][32 * q : 32 * q + 32] = white.reshape(32, 2, ST)

    pl.semaphore_wait(barrier, ALL)

    for s in range(2):
        to_others(lambda z, w, s=s: send(asend[s].at[w * STA + z], arecv[s].at[me], s, a_sem.at[s], z, w))
        if s == 0:
            for offset in range(1, STA):
                send(pair_ref, pairs.at[me_s], 4, p_sem, column(offset), me_w)
        arecv[s][me] = asend[s][me_w * STA + me_s]
    pairs[me_s, 0, 0] = pair_ref[0, 0]
    pairs[me_s, 0, 1] = pair_ref[0, 1]

    left_lanes = lax.broadcasted_iota(jnp.int32, (WIN, ST), 1) < 64

    def cross(p, s):
        a = pairs[p, 0, 0]
        b = pairs[p, 0, 1]
        a_odd = lax.rem(a, 2) == 1
        b_odd = lax.rem(b, 2) == 1
        left = bands[s, a // 2]
        second = bands[s, b // 2].astype(jnp.float32)
        re, im = second[:WIN], second[WIN:]
        re_roll, im_roll = pltpu.roll(re, 64, 1), pltpu.roll(im, 64, 1)
        re_l, im_l = jnp.where(b_odd, re_roll, re), jnp.where(b_odd, im_roll, im)
        re_r, im_r = jnp.where(b_odd, re, re_roll), jnp.where(b_odd, im, im_roll)
        right = jnp.concatenate(
            [jnp.where(left_lanes, re_l, -im_r), jnp.where(left_lanes, im_l, re_r)], axis=0
        ).astype(jnp.bfloat16)
        prod = lax.dot_general(left, right, (((0,), (0,)), ((), ())), preferred_element_type=jnp.float32)
        prod = jnp.where(a_odd, prod[64:], prod[:64])
        top, low = prod[:32], prod[32:]
        return jnp.where(left_lanes, top, pltpu.roll(low, 64, 1)), jnp.where(left_lanes, pltpu.roll(top, 64, 1), low)

    def encode(p, s, parts):
        largest = jnp.maximum(jnp.abs(parts[0]), jnp.abs(parts[1]))
        exponent = jnp.floor(jnp.log(jnp.maximum(largest, 1e-30)) * (1.0 / math.log(2.0))) + 1.0
        scale = jnp.exp2(11.0 - exponent)
        exponent = exponent.astype(jnp.int32) + 128
        for c, v in enumerate(parts):
            value = jnp.clip(jnp.round(v * scale), -2047.0, 2047.0).astype(jnp.int32)
            codes[pl.ds(c, WIN, stride=2), :] = value * 16 + (jnp.right_shift(exponent, 4 * c) & 15)
        csend[s][pl.ds(WIN * p, WIN)] = codes[:64, :].astype(jnp.int16).reshape(WIN, 2, ST)

    for s in range(2):
        wait(arecv[s].at[pl.ds(0, ALL - 1)], a_sem.at[s])
        for z in range(STA):
            part = arecv[s][WIN * z : WIN * z + WIN].astype(jnp.float32)
            rows[64 * z : 64 * z + 64, :] = part.reshape(2 * WIN, ST)
        for z in range(STA):
            for c in range(2):
                part = rows[pl.ds(64 * z + c, WIN, stride=2), :]
                bands[s, z, WIN * c : WIN * c + WIN, :] = part.astype(jnp.bfloat16)
        if s == 0:
            wait(pairs.at[pl.ds(0, STA - 1)], p_sem)
        for offsets in FAR_FIRST:
            for offset in offsets:
                p = column(offset)
                encode(p, s, cross(p, s))

                def step(i, _, p=p, offset=offset, s=s):
                    w = lax.rem(me_w + (20 if offset else 1) + i, WIN)
                    send(csend[s].at[p * WIN + w], crecv[s].at[me], 2 + s, c_sem.at[s], p, w)
                    return 0

                lax.fori_loop(0, WIN if offset else WIN - 1, step, 0)
        crecv[s][me] = csend[s][me]

    t_copies[2].wait()
    wait(pairs.at[pl.ds(0, STA - 1)], send_sem.at[4])
    for s in range(2):
        wait(asend[s].at[pl.ds(0, ALL - 1)], send_sem.at[s])

    for s in range(2):
        wait(crecv[s].at[pl.ds(0, ALL - 1)], c_sem.at[s])
        for z in range(STA):
            part = crecv[s][WIN * z : WIN * z + WIN].astype(jnp.int32)
            codes[64 * z : 64 * z + 64, :] = part.reshape(2 * WIN, ST)
        coded = [codes[pl.ds(c, ALL, stride=2), :] for c in range(2)]
        exponent = (coded[0] & 15) | jnp.left_shift(coded[1] & 15, 4)
        scale = jnp.exp2((exponent - 139).astype(jnp.float32))
        value = jnp.concatenate([jnp.right_shift(v, 4).astype(jnp.float32) * scale for v in coded], axis=0)
        high = value.astype(jnp.bfloat16)
        low = (value - high.astype(jnp.float32)).astype(jnp.bfloat16)
        both = jnp.concatenate([high, low], axis=1)

        for t in range(LAGS // 128):
            row = 128 * t
            value = jnp.zeros((128, 2 * ST), jnp.float32)
            extra = jnp.zeros((128, ST), jnp.float32)
            for block in range(2):
                first = 2 * LAGS * (2 * s + block) + row
                part = both[256 * block : 256 * block + 256]
                value += jnp.dot(lag_v[first : first + 128, :], part, preferred_element_type=jnp.float32)
                extra += jnp.dot(
                    lag_v[first + LAGS : first + LAGS + 128, :], part[:, :ST], preferred_element_type=jnp.float32
                )
            value = value[:, :ST] + (value[:, ST:] + extra)
            if s == 0:
                total[row : row + 128, :] = value
                continue
            value = jnp.transpose(value + total[row : row + 128, :])
            for i2 in range(2):
                for j2 in range(2):
                    part = value[(2 * i2 + j2) * 32 : (2 * i2 + j2) * 32 + 32]
                    order[pl.ds(row + i2 * 64 + j2, 32, stride=2), :] = part
            out_ref[:, :, row : row + 128] = order[row : row + 128, :].reshape(2, 64, 128)
        wait(csend[s].at[pl.ds(0, ALL - 1)], send_sem.at[2 + s])


def body(traces, pair_blocks):
    table = jnp.asarray(tables())
    f32, bf16, i16 = jnp.float32, jnp.bfloat16, jnp.int16
    hbm = pl.BlockSpec(memory_space=pltpu.HBM)
    out = pl.pallas_call(
        kernel,
        out_shape=jax.ShapeDtypeStruct((2, 64, LAGS), f32),
        in_specs=[hbm, pl.BlockSpec(memory_space=pltpu.SMEM), hbm],
        out_specs=pl.BlockSpec(memory_space=pltpu.VMEM),
        scratch_shapes=[
            pltpu.VMEM((ST * SEG, 128), f32),
            pltpu.VMEM((ODD, 256), bf16),
            pltpu.VMEM((FOLD, 256), bf16),
            pltpu.VMEM((8 * LAGS, 256), bf16),
            pltpu.SMEM((STA, 1, 2), jnp.int32),
            pltpu.VMEM((7, 2 * ST, 2 * FOLD), bf16),
            pltpu.VMEM((2, 2 * ST, FOLD), bf16),
            pltpu.VMEM((2 * BANDS, ST), f32),
            pltpu.VMEM((BANDS, ST), f32),
            pltpu.VMEM((2, STA, 2 * WIN, ST), bf16),
            pltpu.VMEM((BANDS, ST), jnp.int32),
            pltpu.VMEM((LAGS, ST), f32),
            pltpu.VMEM((LAGS, ST), f32),
        ]
        + [pltpu.VMEM((ALL, 2, ST), bf16)] * 4
        + [pltpu.VMEM((ALL, 2, ST), i16)] * 4
        + [
            pltpu.SemaphoreType.DMA((4,)),
            pltpu.SemaphoreType.DMA((3,)),
            pltpu.SemaphoreType.DMA((5,)),
            pltpu.SemaphoreType.DMA,
            pltpu.SemaphoreType.DMA((2,)),
            pltpu.SemaphoreType.DMA((2,)),
        ],
        compiler_params=pltpu.CompilerParams(
            collective_id=0, has_side_effects=True, vmem_limit_bytes=54 * 1024 * 1024
        ),
        name="noise_correlation",
    )(traces.reshape(ST * SEG, 128), pair_blocks, table)
    return out.reshape(2, 1, 64, LAGS)


def solution(mesh):
    in_specs = (P("sta", "win", None), P("sta", None))
    out_specs = P("win", "sta", None, None)
    return jax.shard_map(body, mesh=mesh, in_specs=in_specs, out_specs=out_specs, check_vma=False)
```

```python
import functools
import math

import jax
import jax.numpy as jnp
import ml_dtypes
import numpy as np
from jax import lax
from jax.experimental import pallas as pl
from jax.experimental.pallas import tpu as pltpu
from jax.sharding import PartitionSpec as P

L = 8192
LAGS = 512
K0 = 256
BANDS = 512
STA = 8
WIN = 32
ST = 128
SEG = 64
RADIX = 16
FOLD = L // RADIX
ODD = 7 * 2 * FOLD
MESH = pl.DeviceIdType.MESH


def bin_of():
    bins = np.zeros((WIN, STA, 2), np.int64)
    for z in range(STA):
        for q in range(1, 8):
            for u in range(4):
                m = 16 + 4 * z + u
                bins[4 * (q - 1) + u, z] = (16 * m + q, 16 * m + 16 - q)
        for half in range(2):
            for u in range(2):
                for s in range(2):
                    bins[28 + 2 * half + u, z, s] = 16 * (16 + 4 * z + 2 * u + s) + 8 * half
    return bins


def split(table):
    high = table.astype(ml_dtypes.bfloat16)
    low = (table - high.astype(np.float64)).astype(ml_dtypes.bfloat16)
    return high, low


@functools.cache
def tables():
    bins = bin_of()
    n = np.arange(FOLD)

    def trig(k):
        angle = 2 * math.pi * ((k * n) % L) / L
        return np.cos(angle), np.sin(angle)

    odd = np.zeros((7, 4, STA, 2, 2, 2 * FOLD))
    for q in range(1, 8):
        for u in range(4):
            for z in range(STA):
                for s in range(2):
                    c, d = trig(bins[4 * (q - 1) + u, z, s])
                    sign = 1.0 if s == 0 else -1.0
                    odd[q - 1, u, z, s, 0] = np.concatenate([c, sign * d])
                    odd[q - 1, u, z, s, 1] = np.concatenate([-d, sign * c])
    even = np.zeros((2, 2, STA, 2, 2, FOLD))
    for half in range(2):
        for u in range(2):
            for z in range(STA):
                for s in range(2):
                    c, d = trig(bins[28 + 2 * half + u, z, s])
                    even[half, u, z, s, 0] = c
                    even[half, u, z, s, 1] = -d
    shifts = (np.arange(LAGS) - LAGS // 2) % L
    angle = 2 * math.pi * ((bins[..., None] * shifts) % L) / L
    lag = np.stack([np.cos(angle), -np.sin(angle)], axis=3)
    lag = lag.transpose(2, 3, 1, 0, 4).reshape(2 * BANDS, LAGS).T * float(WIN * BANDS) ** (-0.5)
    odd = np.concatenate(split(odd.transpose(0, 3, 1, 2, 4, 5).reshape(7, 128, 2 * FOLD).transpose(0, 2, 1)), axis=2).reshape(ODD, 256)
    even = np.concatenate(split(even.transpose(3, 0, 1, 2, 4, 5).reshape(128, FOLD).T), axis=1)
    lag = np.concatenate(split(lag), axis=0).reshape(2 * LAGS, 4, 256).transpose(1, 0, 2).reshape(8 * LAGS, 256)
    return np.concatenate([odd, even, lag], axis=0)


def fold16(x):
    r2 = math.sqrt(0.5)
    c1 = math.cos(math.pi / 8)
    c3 = math.sin(math.pi / 8)
    e = [x[a] + x[a + 8] for a in range(8)]
    o = [x[a] - x[a + 8] for a in range(8)]
    f = [e[a] + e[a + 4] for a in range(4)]
    g = [e[a] - e[a + 4] for a in range(4)]
    f02, f13 = f[0] + f[2], f[1] + f[3]
    gd, gs = r2 * (g[1] - g[3]), r2 * (g[1] + g[3])
    d = [None] + [o[a] - o[8 - a] for a in range(1, 4)]
    s = [None] + [o[a] + o[8 - a] for a in range(1, 4)]
    d2, s2 = r2 * d[2], r2 * s[2]
    p, m = o[0] + d2, o[0] - d2
    u, v = c1 * d[1] + c3 * d[3], c3 * d[1] - c1 * d[3]
    pp, mm = s2 + o[4], s2 - o[4]
    uu, vv = c3 * s[1] + c1 * s[3], c1 * s[1] - c3 * s[3]
    real = [f02 + f13, p + u, g[0] + gd, m + v, f[0] - f[2], m - v, g[0] - gd, p - u, f02 - f13]
    imag = [None, -(uu + pp), -(g[2] + gs), -(vv + mm), f[3] - f[1], mm - vv, g[2] - gs, pp - uu]
    return real, imag


FAR_FIRST = ((4,), (3, 5), (2, 6), (1, 7), (0,))
ALL = STA * WIN


def kernel(
    x_ref, pair_ref, table_ref, out_ref,
    x_v, odd_v, even_v, lag_v, pairs, fodd, feven, spec, rows, bands, codes, total, order,
    asend_0, asend_1, arecv_0, arecv_1, csend_0, csend_1, crecv_0, crecv_1,
    x_sem, t_sem, send_sem, p_sem, a_sem, c_sem,
):
    me_s = lax.axis_index("sta")
    me_w = lax.axis_index("win")
    me = me_s * WIN + me_w
    asend, arecv = (asend_0, asend_1), (arecv_0, arecv_1)
    csend, crecv = (csend_0, csend_1), (crecv_0, crecv_1)

    x_copies = [
        pltpu.make_async_copy(x_ref.at[pl.ds(2048 * i, 2048)], x_v.at[pl.ds(2048 * i, 2048)], x_sem.at[i])
        for i in range(4)
    ]
    t_copies = [
        pltpu.make_async_copy(table_ref.at[pl.ds(first, dst.shape[0])], dst, t_sem.at[i])
        for i, (first, dst) in enumerate(((0, odd_v), (ODD, even_v), (ODD + FOLD, lag_v)))
    ]
    for copy in x_copies + t_copies[:2]:
        copy.start()

    def column(offset):
        return lax.rem(me_s + offset, STA)

    def to_others(action):
        def in_columns(offsets):
            def step(i, _):
                w = lax.rem(me_w + (1 if 0 in offsets else 20) + i, WIN)
                for offset in offsets:
                    action(column(offset), w)
                return 0

            lax.fori_loop(0, WIN - 1 if 0 in offsets else WIN, step, 0)

        for offsets in FAR_FIRST:
            in_columns(offsets)

    barrier = pltpu.get_barrier_semaphore()

    def greet(offset, i):
        w = lax.rem(me_w + i, WIN)
        pl.semaphore_signal(barrier, inc=1, device_id={"sta": column(offset), "win": w}, device_id_type=MESH)

    def greet_early(i, _):
        for offset in (4, 3, 5):
            greet(offset, i)
        return 0

    lax.fori_loop(0, WIN, greet_early, 0)

    def send(src, dst, phase, recv_sem, z, w):
        pltpu.make_async_remote_copy(
            src_ref=src, dst_ref=dst, send_sem=send_sem.at[phase], recv_sem=recv_sem,
            device_id={"sta": z, "win": w}, device_id_type=MESH,
        ).start()

    def wait(ref, sem):
        pltpu.make_async_copy(ref, ref, sem).wait()

    for chunk in range(4):
        x_copies[chunk].wait()

        def fold(t, _, chunk=chunk):
            if chunk < 2:
                for offset in (2, 6, 1, 7, 0):
                    for i in range(2):
                        greet(offset, 16 * chunk + 2 * t + i)
            lane_tile = lax.rem(t, 4)
            i2 = t // 4
            first = chunk * 2048 + i2 * 64
            x = [x_v[pl.ds(first + 4 * a + lane_tile, 16, stride=128), :] for a in range(RADIX)]
            real, imag = fold16(x)
            row = pl.multiple_of((chunk // 2) * 64 + i2 * 32 + (chunk % 2) * 16, 16)
            lane = pl.multiple_of(lane_tile * 128, 128)

            def put(dst, at, value):
                high = value.astype(jnp.bfloat16)
                low = (value - high.astype(jnp.float32)).astype(jnp.bfloat16)
                dst[pl.ds(row, 16), pl.ds(at, 128)] = high
                dst[pl.ds(row + 128, 16), pl.ds(at, 128)] = low

            put(feven.at[0], lane, real[0])
            put(feven.at[1], lane, real[8])
            for q in range(1, 8):
                put(fodd.at[q - 1], lane, real[q])
                put(fodd.at[q - 1], pl.multiple_of(lane + FOLD, 128), imag[q])
            return 0

        lax.fori_loop(0, 8, fold, 0)

    def dft(data, table):
        prod = jnp.dot(data, table, preferred_element_type=jnp.float32)
        return prod[:ST, :128] + (prod[:ST, 128:] + prod[ST:, :128])

    t_copies[0].wait()
    t_copies[1].wait()
    t_copies[2].start()
    power = jnp.zeros((8, ST), jnp.float32)
    for q in range(8):
        if q < 7:
            value = dft(fodd[q], odd_v[1024 * q : 1024 * q + 1024])
        else:
            first_half = lax.rem(lax.broadcasted_iota(jnp.int32, (ST, 128), 1), 64) < 32
            value = jnp.where(first_half, dft(feven[0], even_v[...]), dft(feven[1], even_v[...]))
        value = jnp.transpose(value)
        spec[128 * q : 128 * q + 128, :] = value
        power = power + jnp.sum((value * value).reshape(16, 8, ST), axis=0)
    mean = jnp.sum(power, axis=0, keepdims=True) * (1.0 / BANDS)
    inverse = 1.0 / jnp.sqrt(mean + 1e-06)
    for q in range(8):
        for s in range(2):
            first = 128 * q + 64 * s
            white = (spec[first : first + 64, :] * inverse).astype(jnp.bfloat16)
            asend[s][32 * q : 32 * q + 32] = white.reshape(32, 2, ST)

    pl.semaphore_wait(barrier, ALL)

    for s in range(2):
        to_others(lambda z, w, s=s: send(asend[s].at[w * STA + z], arecv[s].at[me], s, a_sem.at[s], z, w))
        if s == 0:
            for offset in range(1, STA):
                send(pair_ref, pairs.at[me_s], 4, p_sem, column(offset), me_w)
        arecv[s][me] = asend[s][me_w * STA + me_s]
    pairs[me_s, 0, 0] = pair_ref[0, 0]
    pairs[me_s, 0, 1] = pair_ref[0, 1]

    left_lanes = lax.broadcasted_iota(jnp.int32, (WIN, ST), 1) < 64

    def cross(p, s):
        a = pairs[p, 0, 0]
        b = pairs[p, 0, 1]
        a_odd = lax.rem(a, 2) == 1
        b_odd = lax.rem(b, 2) == 1
        left = bands[s, a // 2]
        second = bands[s, b // 2].astype(jnp.float32)
        re, im = second[:WIN], second[WIN:]
        re_roll, im_roll = pltpu.roll(re, 64, 1), pltpu.roll(im, 64, 1)
        re_l, im_l = jnp.where(b_odd, re_roll, re), jnp.where(b_odd, im_roll, im)
        re_r, im_r = jnp.where(b_odd, re, re_roll), jnp.where(b_odd, im, im_roll)
        right = jnp.concatenate(
            [jnp.where(left_lanes, re_l, -im_r), jnp.where(left_lanes, im_l, re_r)], axis=0
        ).astype(jnp.bfloat16)
        prod = lax.dot_general(left, right, (((0,), (0,)), ((), ())), preferred_element_type=jnp.float32)
        prod = jnp.where(a_odd, prod[64:], prod[:64])
        top, low = prod[:32], prod[32:]
        return jnp.where(left_lanes, top, pltpu.roll(low, 64, 1)), jnp.where(left_lanes, pltpu.roll(top, 64, 1), low)

    def encode(p, s, parts):
        largest = jnp.maximum(jnp.abs(parts[0]), jnp.abs(parts[1]))
        exponent = jnp.floor(jnp.log(jnp.maximum(largest, 1e-30)) * (1.0 / math.log(2.0))) + 1.0
        scale = jnp.exp2(11.0 - exponent)
        exponent = exponent.astype(jnp.int32) + 128
        for c, v in enumerate(parts):
            value = jnp.clip(jnp.round(v * scale), -2047.0, 2047.0).astype(jnp.int32)
            codes[pl.ds(c, WIN, stride=2), :] = value * 16 + (jnp.right_shift(exponent, 4 * c) & 15)
        csend[s][pl.ds(WIN * p, WIN)] = codes[:64, :].astype(jnp.int16).reshape(WIN, 2, ST)

    for s in range(2):
        wait(arecv[s].at[pl.ds(0, ALL - 1)], a_sem.at[s])
        for z in range(STA):
            part = arecv[s][WIN * z : WIN * z + WIN].astype(jnp.float32)
            rows[64 * z : 64 * z + 64, :] = part.reshape(2 * WIN, ST)
        for z in range(STA):
            for c in range(2):
                part = rows[pl.ds(64 * z + c, WIN, stride=2), :]
                bands[s, z, WIN * c : WIN * c + WIN, :] = part.astype(jnp.bfloat16)
        if s == 0:
            wait(pairs.at[pl.ds(0, STA - 1)], p_sem)
        for offsets in FAR_FIRST:
            pairs_now = [column(offset) for offset in offsets]
            for p in pairs_now:
                encode(p, s, cross(p, s))

            def step(i, _, pairs_now=pairs_now, here=0 in offsets, s=s):
                w = lax.rem(me_w + (1 if here else 20) + i, WIN)
                for p in pairs_now:
                    send(csend[s].at[p * WIN + w], crecv[s].at[me], 2 + s, c_sem.at[s], p, w)
                return 0

            lax.fori_loop(0, WIN - 1 if 0 in offsets else WIN, step, 0)
        crecv[s][me] = csend[s][me]

    t_copies[2].wait()
    wait(pairs.at[pl.ds(0, STA - 1)], send_sem.at[4])
    for s in range(2):
        wait(asend[s].at[pl.ds(0, ALL - 1)], send_sem.at[s])

    for s in range(2):
        wait(crecv[s].at[pl.ds(0, ALL - 1)], c_sem.at[s])
        for z in range(STA):
            part = crecv[s][WIN * z : WIN * z + WIN].astype(jnp.int32)
            codes[64 * z : 64 * z + 64, :] = part.reshape(2 * WIN, ST)
        coded = [codes[pl.ds(c, ALL, stride=2), :] for c in range(2)]
        exponent = (coded[0] & 15) | jnp.left_shift(coded[1] & 15, 4)
        scale = jnp.exp2((exponent - 139).astype(jnp.float32))
        value = jnp.concatenate([jnp.right_shift(v, 4).astype(jnp.float32) * scale for v in coded], axis=0)
        high = value.astype(jnp.bfloat16)
        low = (value - high.astype(jnp.float32)).astype(jnp.bfloat16)
        both = jnp.concatenate([high, low], axis=1)

        for t in range(LAGS // 128):
            row = 128 * t
            value = jnp.zeros((128, 2 * ST), jnp.float32)
            extra = jnp.zeros((128, ST), jnp.float32)
            for block in range(2):
                first = 2 * LAGS * (2 * s + block) + row
                part = both[256 * block : 256 * block + 256]
                value += jnp.dot(lag_v[first : first + 128, :], part, preferred_element_type=jnp.float32)
                extra += jnp.dot(
                    lag_v[first + LAGS : first + LAGS + 128, :], part[:, :ST], preferred_element_type=jnp.float32
                )
            value = value[:, :ST] + (value[:, ST:] + extra)
            if s == 0:
                total[row : row + 128, :] = value
                continue
            value = jnp.transpose(value + total[row : row + 128, :])
            for i2 in range(2):
                for j2 in range(2):
                    part = value[(2 * i2 + j2) * 32 : (2 * i2 + j2) * 32 + 32]
                    order[pl.ds(row + i2 * 64 + j2, 32, stride=2), :] = part
            out_ref[:, :, row : row + 128] = order[row : row + 128, :].reshape(2, 64, 128)
        wait(csend[s].at[pl.ds(0, ALL - 1)], send_sem.at[2 + s])


def body(traces, pair_blocks):
    table = jnp.asarray(tables())
    f32, bf16, i16 = jnp.float32, jnp.bfloat16, jnp.int16
    hbm = pl.BlockSpec(memory_space=pltpu.HBM)
    out = pl.pallas_call(
        kernel,
        out_shape=jax.ShapeDtypeStruct((2, 64, LAGS), f32),
        in_specs=[hbm, pl.BlockSpec(memory_space=pltpu.SMEM), hbm],
        out_specs=pl.BlockSpec(memory_space=pltpu.VMEM),
        scratch_shapes=[
            pltpu.VMEM((ST * SEG, 128), f32),
            pltpu.VMEM((ODD, 256), bf16),
            pltpu.VMEM((FOLD, 256), bf16),
            pltpu.VMEM((8 * LAGS, 256), bf16),
            pltpu.SMEM((STA, 1, 2), jnp.int32),
            pltpu.VMEM((7, 2 * ST, 2 * FOLD), bf16),
            pltpu.VMEM((2, 2 * ST, FOLD), bf16),
            pltpu.VMEM((2 * BANDS, ST), f32),
            pltpu.VMEM((BANDS, ST), f32),
            pltpu.VMEM((2, STA, 2 * WIN, ST), bf16),
            pltpu.VMEM((BANDS, ST), jnp.int32),
            pltpu.VMEM((LAGS, ST), f32),
            pltpu.VMEM((LAGS, ST), f32),
        ]
        + [pltpu.VMEM((ALL, 2, ST), bf16)] * 4
        + [pltpu.VMEM((ALL, 2, ST), i16)] * 4
        + [
            pltpu.SemaphoreType.DMA((4,)),
            pltpu.SemaphoreType.DMA((3,)),
            pltpu.SemaphoreType.DMA((5,)),
            pltpu.SemaphoreType.DMA,
            pltpu.SemaphoreType.DMA((2,)),
            pltpu.SemaphoreType.DMA((2,)),
        ],
        compiler_params=pltpu.CompilerParams(
            collective_id=0, has_side_effects=True, vmem_limit_bytes=52 * 1024 * 1024
        ),
        name="noise_correlation",
    )(traces.reshape(ST * SEG, 128), pair_blocks, table)
    return out.reshape(2, 1, 64, LAGS)


def solution(mesh):
    in_specs = (P("sta", "win", None), P("sta", None))
    out_specs = P("win", "sta", None, None)
    return jax.shard_map(body, mesh=mesh, in_specs=in_specs, out_specs=out_specs, check_vma=False)
```

```python
import functools
import math

import jax
import jax.numpy as jnp
import ml_dtypes
import numpy as np
from jax import lax
from jax.experimental import pallas as pl
from jax.experimental.pallas import tpu as pltpu
from jax.sharding import PartitionSpec as P

L = 8192
LAGS = 512
K0 = 256
BANDS = 512
STA = 8
WIN = 32
ST = 128
SEG = 64
RADIX = 16
FOLD = L // RADIX
ODD = 7 * 2 * FOLD
MESH = pl.DeviceIdType.MESH


def bin_of():
    bins = np.zeros((WIN, STA, 2), np.int64)
    for z in range(STA):
        for q in range(1, 8):
            for u in range(4):
                m = 16 + 4 * z + u
                bins[4 * (q - 1) + u, z] = (16 * m + q, 16 * m + 16 - q)
        for half in range(2):
            for u in range(2):
                for s in range(2):
                    bins[28 + 2 * half + u, z, s] = 16 * (16 + 4 * z + 2 * u + s) + 8 * half
    return bins


def split(table):
    high = table.astype(ml_dtypes.bfloat16)
    low = (table - high.astype(np.float64)).astype(ml_dtypes.bfloat16)
    return high, low


@functools.cache
def tables():
    bins = bin_of()
    n = np.arange(FOLD)

    def trig(k):
        angle = 2 * math.pi * ((k * n) % L) / L
        return np.cos(angle), np.sin(angle)

    odd = np.zeros((7, 4, STA, 2, 2, 2 * FOLD))
    for q in range(1, 8):
        for u in range(4):
            for z in range(STA):
                for s in range(2):
                    c, d = trig(bins[4 * (q - 1) + u, z, s])
                    sign = 1.0 if s == 0 else -1.0
                    odd[q - 1, u, z, s, 0] = np.concatenate([c, sign * d])
                    odd[q - 1, u, z, s, 1] = np.concatenate([-d, sign * c])
    even = np.zeros((2, 2, STA, 2, 2, FOLD))
    for half in range(2):
        for u in range(2):
            for z in range(STA):
                for s in range(2):
                    c, d = trig(bins[28 + 2 * half + u, z, s])
                    even[half, u, z, s, 0] = c
                    even[half, u, z, s, 1] = -d
    shifts = (np.arange(LAGS) - LAGS // 2) % L
    angle = 2 * math.pi * ((bins[..., None] * shifts) % L) / L
    lag = np.stack([np.cos(angle), -np.sin(angle)], axis=3)
    lag = lag.transpose(2, 3, 1, 0, 4).reshape(2 * BANDS, LAGS).T * float(WIN * BANDS) ** (-0.5)
    odd = np.concatenate(split(odd.transpose(0, 3, 1, 2, 4, 5).reshape(7, 128, 2 * FOLD).transpose(0, 2, 1)), axis=2).reshape(ODD, 256)
    even = np.concatenate(split(even.transpose(3, 0, 1, 2, 4, 5).reshape(128, FOLD).T), axis=1)
    lag = np.concatenate(split(lag), axis=0).reshape(2 * LAGS, 4, 256).transpose(1, 0, 2).reshape(8 * LAGS, 256)
    return np.concatenate([odd, even, lag], axis=0)


def fold16(x):
    r2 = math.sqrt(0.5)
    c1 = math.cos(math.pi / 8)
    c3 = math.sin(math.pi / 8)
    e = [x[a] + x[a + 8] for a in range(8)]
    o = [x[a] - x[a + 8] for a in range(8)]
    f = [e[a] + e[a + 4] for a in range(4)]
    g = [e[a] - e[a + 4] for a in range(4)]
    f02, f13 = f[0] + f[2], f[1] + f[3]
    gd, gs = r2 * (g[1] - g[3]), r2 * (g[1] + g[3])
    d = [None] + [o[a] - o[8 - a] for a in range(1, 4)]
    s = [None] + [o[a] + o[8 - a] for a in range(1, 4)]
    d2, s2 = r2 * d[2], r2 * s[2]
    p, m = o[0] + d2, o[0] - d2
    u, v = c1 * d[1] + c3 * d[3], c3 * d[1] - c1 * d[3]
    pp, mm = s2 + o[4], s2 - o[4]
    uu, vv = c3 * s[1] + c1 * s[3], c1 * s[1] - c3 * s[3]
    real = [f02 + f13, p + u, g[0] + gd, m + v, f[0] - f[2], m - v, g[0] - gd, p - u, f02 - f13]
    imag = [None, -(uu + pp), -(g[2] + gs), -(vv + mm), f[3] - f[1], mm - vv, g[2] - gs, pp - uu]
    return real, imag


FAR_FIRST = ((4,), (3, 5), (2, 6), (1, 7), (0,))
ALL = STA * WIN


def kernel(
    x_ref, pair_ref, table_ref, out_ref,
    x_v, odd_v, even_v, lag_v, pairs, fodd, feven, spec, rows, bands, codes, total, order,
    asend_0, asend_1, arecv_0, arecv_1, csend_0, csend_1, crecv_0, crecv_1,
    x_sem, t_sem, send_sem, p_sem, a_sem, c_sem,
):
    me_s = lax.axis_index("sta")
    me_w = lax.axis_index("win")
    me = me_s * WIN + me_w
    asend, arecv = (asend_0, asend_1), (arecv_0, arecv_1)
    csend, crecv = (csend_0, csend_1), (crecv_0, crecv_1)

    x_copies = [
        pltpu.make_async_copy(x_ref.at[pl.ds(2048 * i, 2048)], x_v.at[pl.ds(2048 * i, 2048)], x_sem.at[i])
        for i in range(4)
    ]
    t_copies = [
        pltpu.make_async_copy(table_ref.at[pl.ds(first, dst.shape[0])], dst, t_sem.at[i])
        for i, (first, dst) in enumerate(((0, odd_v), (ODD, even_v), (ODD + FOLD, lag_v)))
    ]
    for copy in x_copies + t_copies[:2]:
        copy.start()

    def column(offset):
        return lax.rem(me_s + offset, STA)

    row = me_w // 8
    near = [lax.rem(lax.rem(me_w, 8) + i, 8) for i in (4, 5, 3, 2, 6, 7, 1, 0)]

    def in_columns(offsets, action):
        columns = [column(offset) for offset in offsets]

        def step(i, _):
            base = lax.rem(row + 2 + i, 4) * 8
            for w in near:
                for z in columns:
                    action(z, base + w)
            return 0

        if 0 not in offsets:
            lax.fori_loop(0, 4, step, 0)
            return
        lax.fori_loop(0, 2, step, 0)
        lax.fori_loop(3, 4, step, 0)
        for w in near[:-1]:
            action(columns[0], row * 8 + w)

    def to_others(action):
        for offsets in FAR_FIRST:
            in_columns(offsets, action)

    barrier = pltpu.get_barrier_semaphore()

    def greet(z, w):
        pl.semaphore_signal(barrier, inc=1, device_id={"sta": z, "win": w}, device_id_type=MESH)

    to_others(greet)

    def send(src, dst, phase, recv_sem, z, w):
        pltpu.make_async_remote_copy(
            src_ref=src, dst_ref=dst, send_sem=send_sem.at[phase], recv_sem=recv_sem,
            device_id={"sta": z, "win": w}, device_id_type=MESH,
        ).start()

    def wait(ref, sem):
        pltpu.make_async_copy(ref, ref, sem).wait()

    for chunk in range(4):
        x_copies[chunk].wait()

        def fold(t, _, chunk=chunk):
            lane_tile = lax.rem(t, 4)
            i2 = t // 4
            first = chunk * 2048 + i2 * 64
            x = [x_v[pl.ds(first + 4 * a + lane_tile, 16, stride=128), :] for a in range(RADIX)]
            real, imag = fold16(x)
            row = pl.multiple_of((chunk // 2) * 64 + i2 * 32 + (chunk % 2) * 16, 16)
            lane = pl.multiple_of(lane_tile * 128, 128)

            def put(dst, at, value):
                high = value.astype(jnp.bfloat16)
                low = (value - high.astype(jnp.float32)).astype(jnp.bfloat16)
                dst[pl.ds(row, 16), pl.ds(at, 128)] = high
                dst[pl.ds(row + 128, 16), pl.ds(at, 128)] = low

            put(feven.at[0], lane, real[0])
            put(feven.at[1], lane, real[8])
            for q in range(1, 8):
                put(fodd.at[q - 1], lane, real[q])
                put(fodd.at[q - 1], pl.multiple_of(lane + FOLD, 128), imag[q])
            return 0

        lax.fori_loop(0, 8, fold, 0)

    def dft(data, table):
        prod = jnp.dot(data, table, preferred_element_type=jnp.float32)
        return prod[:ST, :128] + (prod[:ST, 128:] + prod[ST:, :128])

    t_copies[0].wait()
    t_copies[1].wait()
    t_copies[2].start()
    power = jnp.zeros((8, ST), jnp.float32)
    for q in range(8):
        if q < 7:
            value = dft(fodd[q], odd_v[1024 * q : 1024 * q + 1024])
        else:
            first_half = lax.rem(lax.broadcasted_iota(jnp.int32, (ST, 128), 1), 64) < 32
            value = jnp.where(first_half, dft(feven[0], even_v[...]), dft(feven[1], even_v[...]))
        value = jnp.transpose(value)
        spec[128 * q : 128 * q + 128, :] = value
        power = power + jnp.sum((value * value).reshape(16, 8, ST), axis=0)
    mean = jnp.sum(power, axis=0, keepdims=True) * (1.0 / BANDS)
    inverse = 1.0 / jnp.sqrt(mean + 1e-06)
    def whiten(s):
        for q in range(8):
            first = 128 * q + 64 * s
            white = (spec[first : first + 64, :] * inverse).astype(jnp.bfloat16)
            asend[s][32 * q : 32 * q + 32] = white.reshape(32, 2, ST)

    whiten(0)
    pl.semaphore_wait(barrier, ALL - 1)

    for s in range(2):
        if s == 1:
            whiten(1)
        to_others(lambda z, w, s=s: send(asend[s].at[w * STA + z], arecv[s].at[me], s, a_sem.at[s], z, w))
        if s == 0:
            for offset in range(1, STA):
                send(pair_ref, pairs.at[me_s], 4, p_sem, column(offset), me_w)
        arecv[s][me] = asend[s][me_w * STA + me_s]
    pairs[me_s, 0, 0] = pair_ref[0, 0]
    pairs[me_s, 0, 1] = pair_ref[0, 1]

    left_lanes = lax.broadcasted_iota(jnp.int32, (WIN, ST), 1) < 64

    def cross(p, s):
        a = pairs[p, 0, 0]
        b = pairs[p, 0, 1]
        a_odd = lax.rem(a, 2) == 1
        b_odd = lax.rem(b, 2) == 1
        left = bands[s, a // 2]
        second = bands[s, b // 2].astype(jnp.float32)
        re, im = second[:WIN], second[WIN:]
        re_roll, im_roll = pltpu.roll(re, 64, 1), pltpu.roll(im, 64, 1)
        re_l, im_l = jnp.where(b_odd, re_roll, re), jnp.where(b_odd, im_roll, im)
        re_r, im_r = jnp.where(b_odd, re, re_roll), jnp.where(b_odd, im, im_roll)
        right = jnp.concatenate(
            [jnp.where(left_lanes, re_l, -im_r), jnp.where(left_lanes, im_l, re_r)], axis=0
        ).astype(jnp.bfloat16)
        prod = lax.dot_general(left, right, (((0,), (0,)), ((), ())), preferred_element_type=jnp.float32)
        prod = jnp.where(a_odd, prod[64:], prod[:64])
        top, low = prod[:32], prod[32:]
        return jnp.where(left_lanes, top, pltpu.roll(low, 64, 1)), jnp.where(left_lanes, pltpu.roll(top, 64, 1), low)

    def encode(p, s, parts):
        largest = jnp.maximum(jnp.abs(parts[0]), jnp.abs(parts[1]))
        exponent = jnp.floor(jnp.log(jnp.maximum(largest, 1e-30)) * (1.0 / math.log(2.0))) + 1.0
        scale = jnp.exp2(11.0 - exponent)
        exponent = exponent.astype(jnp.int32) + 128
        for c, v in enumerate(parts):
            value = jnp.clip(jnp.round(v * scale), -2047.0, 2047.0).astype(jnp.int32)
            codes[pl.ds(c, WIN, stride=2), :] = value * 16 + (jnp.right_shift(exponent, 4 * c) & 15)
        csend[s][pl.ds(WIN * p, WIN)] = codes[:64, :].astype(jnp.int16).reshape(WIN, 2, ST)

    for s in range(2):
        wait(arecv[s].at[pl.ds(0, ALL - 1)], a_sem.at[s])
        for z in range(STA):
            part = arecv[s][WIN * z : WIN * z + WIN].astype(jnp.float32)
            rows[64 * z : 64 * z + 64, :] = part.reshape(2 * WIN, ST)
        for z in range(STA):
            for c in range(2):
                part = rows[pl.ds(64 * z + c, WIN, stride=2), :]
                bands[s, z, WIN * c : WIN * c + WIN, :] = part.astype(jnp.bfloat16)
        if s == 0:
            wait(pairs.at[pl.ds(0, STA - 1)], p_sem)
        for offsets in FAR_FIRST:
            pairs_now = [column(offset) for offset in offsets]
            for p in pairs_now:
                encode(p, s, cross(p, s))

            in_columns(
                offsets, lambda p, w, s=s: send(csend[s].at[p * WIN + w], crecv[s].at[me], 2 + s, c_sem.at[s], p, w)
            )
        crecv[s][me] = csend[s][me]

    t_copies[2].wait()
    wait(pairs.at[pl.ds(0, STA - 1)], send_sem.at[4])
    for s in range(2):
        wait(asend[s].at[pl.ds(0, ALL - 1)], send_sem.at[s])

    for s in range(2):
        wait(crecv[s].at[pl.ds(0, ALL - 1)], c_sem.at[s])
        for z in range(STA):
            part = crecv[s][WIN * z : WIN * z + WIN].astype(jnp.int32)
            codes[64 * z : 64 * z + 64, :] = part.reshape(2 * WIN, ST)
        coded = [codes[pl.ds(c, ALL, stride=2), :] for c in range(2)]
        exponent = (coded[0] & 15) | jnp.left_shift(coded[1] & 15, 4)
        scale = jnp.exp2((exponent - 139).astype(jnp.float32))
        value = jnp.concatenate([jnp.right_shift(v, 4).astype(jnp.float32) * scale for v in coded], axis=0)
        high = value.astype(jnp.bfloat16)
        low = (value - high.astype(jnp.float32)).astype(jnp.bfloat16)
        both = jnp.concatenate([high, low], axis=1)

        for t in range(LAGS // 128):
            row = 128 * t
            value = jnp.zeros((128, 2 * ST), jnp.float32)
            extra = jnp.zeros((128, ST), jnp.float32)
            for block in range(2):
                first = 2 * LAGS * (2 * s + block) + row
                part = both[256 * block : 256 * block + 256]
                value += jnp.dot(lag_v[first : first + 128, :], part, preferred_element_type=jnp.float32)
                extra += jnp.dot(
                    lag_v[first + LAGS : first + LAGS + 128, :], part[:, :ST], preferred_element_type=jnp.float32
                )
            value = value[:, :ST] + (value[:, ST:] + extra)
            if s == 0:
                total[row : row + 128, :] = value
                continue
            value = jnp.transpose(value + total[row : row + 128, :])
            for i2 in range(2):
                for j2 in range(2):
                    part = value[(2 * i2 + j2) * 32 : (2 * i2 + j2) * 32 + 32]
                    order[pl.ds(row + i2 * 64 + j2, 32, stride=2), :] = part
            out_ref[:, :, row : row + 128] = order[row : row + 128, :].reshape(2, 64, 128)
        wait(csend[s].at[pl.ds(0, ALL - 1)], send_sem.at[2 + s])


def body(traces, pair_blocks):
    table = jnp.asarray(tables())
    f32, bf16, i16 = jnp.float32, jnp.bfloat16, jnp.int16
    hbm = pl.BlockSpec(memory_space=pltpu.HBM)
    out = pl.pallas_call(
        kernel,
        out_shape=jax.ShapeDtypeStruct((2, 64, LAGS), f32),
        in_specs=[hbm, pl.BlockSpec(memory_space=pltpu.SMEM), hbm],
        out_specs=pl.BlockSpec(memory_space=pltpu.VMEM),
        scratch_shapes=[
            pltpu.VMEM((ST * SEG, 128), f32),
            pltpu.VMEM((ODD, 256), bf16),
            pltpu.VMEM((FOLD, 256), bf16),
            pltpu.VMEM((8 * LAGS, 256), bf16),
            pltpu.SMEM((STA, 1, 2), jnp.int32),
            pltpu.VMEM((7, 2 * ST, 2 * FOLD), bf16),
            pltpu.VMEM((2, 2 * ST, FOLD), bf16),
            pltpu.VMEM((2 * BANDS, ST), f32),
            pltpu.VMEM((BANDS, ST), f32),
            pltpu.VMEM((2, STA, 2 * WIN, ST), bf16),
            pltpu.VMEM((BANDS, ST), jnp.int32),
            pltpu.VMEM((LAGS, ST), f32),
            pltpu.VMEM((LAGS, ST), f32),
        ]
        + [pltpu.VMEM((ALL, 2, ST), bf16)] * 4
        + [pltpu.VMEM((ALL, 2, ST), i16)] * 4
        + [
            pltpu.SemaphoreType.DMA((4,)),
            pltpu.SemaphoreType.DMA((3,)),
            pltpu.SemaphoreType.DMA((5,)),
            pltpu.SemaphoreType.DMA,
            pltpu.SemaphoreType.DMA((2,)),
            pltpu.SemaphoreType.DMA((2,)),
        ],
        compiler_params=pltpu.CompilerParams(
            collective_id=0, has_side_effects=True, vmem_limit_bytes=52 * 1024 * 1024
        ),
        name="noise_correlation",
    )(traces.reshape(ST * SEG, 128), pair_blocks, table)
    return out.reshape(2, 1, 64, LAGS)


def solution(mesh):
    in_specs = (P("sta", "win", None), P("sta", None))
    out_specs = P("win", "sta", None, None)
    return jax.shard_map(body, mesh=mesh, in_specs=in_specs, out_specs=out_specs, check_vma=False)
```

```python
import functools
import math

import jax
import jax.numpy as jnp
import ml_dtypes
import numpy as np
from jax import lax
from jax.experimental import pallas as pl
from jax.experimental.pallas import tpu as pltpu
from jax.sharding import PartitionSpec as P

L = 8192
LAGS = 512
K0 = 256
BANDS = 512
STA = 8
WIN = 32
ST = 128
SEG = 64
RADIX = 16
FOLD = L // RADIX
ODD = 7 * 2 * FOLD
MESH = pl.DeviceIdType.MESH


def bin_of():
    bins = np.zeros((WIN, STA, 2), np.int64)
    for z in range(STA):
        for q in range(1, 8):
            for u in range(4):
                m = 16 + 4 * z + u
                bins[4 * (q - 1) + u, z] = (16 * m + q, 16 * m + 16 - q)
        for half in range(2):
            for u in range(2):
                for s in range(2):
                    bins[28 + 2 * half + u, z, s] = 16 * (16 + 4 * z + 2 * u + s) + 8 * half
    return bins


def split(table):
    high = table.astype(ml_dtypes.bfloat16)
    low = (table - high.astype(np.float64)).astype(ml_dtypes.bfloat16)
    return high, low


@functools.cache
def tables():
    bins = bin_of()
    n = np.arange(FOLD)

    def trig(k):
        angle = 2 * math.pi * ((k * n) % L) / L
        return np.cos(angle), np.sin(angle)

    odd = np.zeros((7, 4, STA, 2, 2, 2 * FOLD))
    for q in range(1, 8):
        for u in range(4):
            for z in range(STA):
                for s in range(2):
                    c, d = trig(bins[4 * (q - 1) + u, z, s])
                    sign = 1.0 if s == 0 else -1.0
                    odd[q - 1, u, z, s, 0] = np.concatenate([c, sign * d])
                    odd[q - 1, u, z, s, 1] = np.concatenate([-d, sign * c])
    even = np.zeros((2, 2, STA, 2, 2, FOLD))
    for half in range(2):
        for u in range(2):
            for z in range(STA):
                for s in range(2):
                    c, d = trig(bins[28 + 2 * half + u, z, s])
                    even[half, u, z, s, 0] = c
                    even[half, u, z, s, 1] = -d
    shifts = (np.arange(LAGS) - LAGS // 2) % L
    angle = 2 * math.pi * ((bins[..., None] * shifts) % L) / L
    lag = np.stack([np.cos(angle), -np.sin(angle)], axis=3)
    lag = lag.transpose(2, 3, 1, 0, 4).reshape(2 * BANDS, LAGS).T * float(WIN * BANDS) ** (-0.5)
    odd = np.concatenate(split(odd.transpose(0, 3, 1, 2, 4, 5).reshape(7, 128, 2 * FOLD).transpose(0, 2, 1)), axis=2).reshape(ODD, 256)
    even = np.concatenate(split(even.transpose(3, 0, 1, 2, 4, 5).reshape(128, FOLD).T), axis=1)
    lag = np.concatenate(split(lag), axis=0).reshape(2 * LAGS, 4, 256).transpose(1, 0, 2).reshape(8 * LAGS, 256)
    return np.concatenate([odd, even, lag], axis=0)


def fold16(x):
    r2 = math.sqrt(0.5)
    c1 = math.cos(math.pi / 8)
    c3 = math.sin(math.pi / 8)
    e = [x[a] + x[a + 8] for a in range(8)]
    o = [x[a] - x[a + 8] for a in range(8)]
    f = [e[a] + e[a + 4] for a in range(4)]
    g = [e[a] - e[a + 4] for a in range(4)]
    f02, f13 = f[0] + f[2], f[1] + f[3]
    gd, gs = r2 * (g[1] - g[3]), r2 * (g[1] + g[3])
    d = [None] + [o[a] - o[8 - a] for a in range(1, 4)]
    s = [None] + [o[a] + o[8 - a] for a in range(1, 4)]
    d2, s2 = r2 * d[2], r2 * s[2]
    p, m = o[0] + d2, o[0] - d2
    u, v = c1 * d[1] + c3 * d[3], c3 * d[1] - c1 * d[3]
    pp, mm = s2 + o[4], s2 - o[4]
    uu, vv = c3 * s[1] + c1 * s[3], c1 * s[1] - c3 * s[3]
    real = [f02 + f13, p + u, g[0] + gd, m + v, f[0] - f[2], m - v, g[0] - gd, p - u, f02 - f13]
    imag = [None, -(uu + pp), -(g[2] + gs), -(vv + mm), f[3] - f[1], mm - vv, g[2] - gs, pp - uu]
    return real, imag


FAR_FIRST = ((4, 3, 5), (2, 6, 1, 7), (0,))
ALL = STA * WIN


def kernel(
    x_ref, pair_ref, table_ref, out_ref,
    x_v, odd_v, even_v, lag_v, pairs, fodd, feven, spec, rows, bands, codes, total, order,
    asend_0, asend_1, arecv_0, arecv_1, csend_0, csend_1, crecv_0, crecv_1,
    x_sem, t_sem, send_sem, p_sem, a_sem, c_sem,
):
    me_s = lax.axis_index("sta")
    me_w = lax.axis_index("win")
    me = me_s * WIN + me_w
    asend, arecv = (asend_0, asend_1), (arecv_0, arecv_1)
    csend, crecv = (csend_0, csend_1), (crecv_0, crecv_1)

    x_copies = [
        pltpu.make_async_copy(x_ref.at[pl.ds(2048 * i, 2048)], x_v.at[pl.ds(2048 * i, 2048)], x_sem.at[i])
        for i in range(4)
    ]
    t_copies = [
        pltpu.make_async_copy(table_ref.at[pl.ds(first, dst.shape[0])], dst, t_sem.at[i])
        for i, (first, dst) in enumerate(((0, odd_v), (ODD, even_v), (ODD + FOLD, lag_v)))
    ]
    for copy in x_copies + t_copies[:2]:
        copy.start()

    def column(offset):
        return lax.rem(me_s + offset, STA)

    row = me_w // 8
    near = [lax.rem(lax.rem(me_w, 8) + i, 8) for i in (4, 5, 3, 2, 6, 7, 1, 0)]

    def in_columns(offsets, action):
        columns = [column(offset) for offset in offsets]

        def step(i, _):
            base = lax.rem(row + 2 + i, 4) * 8
            for w in near:
                for z in columns:
                    action(z, base + w)
            return 0

        if 0 not in offsets:
            lax.fori_loop(0, 4, step, 0)
            return
        lax.fori_loop(0, 2, step, 0)
        lax.fori_loop(3, 4, step, 0)
        for w in near[:-1]:
            action(columns[0], row * 8 + w)

    def to_others(action):
        for offsets in FAR_FIRST:
            in_columns(offsets, action)

    barrier = pltpu.get_barrier_semaphore()

    def greet(z, w):
        pl.semaphore_signal(barrier, inc=1, device_id={"sta": z, "win": w}, device_id_type=MESH)

    to_others(greet)

    def send(src, dst, phase, recv_sem, z, w):
        pltpu.make_async_remote_copy(
            src_ref=src, dst_ref=dst, send_sem=send_sem.at[phase], recv_sem=recv_sem,
            device_id={"sta": z, "win": w}, device_id_type=MESH,
        ).start()

    def wait(ref, sem):
        pltpu.make_async_copy(ref, ref, sem).wait()

    for chunk in range(4):
        x_copies[chunk].wait()

        def fold(t, _, chunk=chunk):
            lane_tile = lax.rem(t, 4)
            i2 = t // 4
            first = chunk * 2048 + i2 * 64
            x = [x_v[pl.ds(first + 4 * a + lane_tile, 16, stride=128), :] for a in range(RADIX)]
            real, imag = fold16(x)
            row = pl.multiple_of((chunk // 2) * 64 + i2 * 32 + (chunk % 2) * 16, 16)
            lane = pl.multiple_of(lane_tile * 128, 128)

            def put(dst, at, value):
                high = value.astype(jnp.bfloat16)
                low = (value - high.astype(jnp.float32)).astype(jnp.bfloat16)
                dst[pl.ds(row, 16), pl.ds(at, 128)] = high
                dst[pl.ds(row + 128, 16), pl.ds(at, 128)] = low

            put(feven.at[0], lane, real[0])
            put(feven.at[1], lane, real[8])
            for q in range(1, 8):
                put(fodd.at[q - 1], lane, real[q])
                put(fodd.at[q - 1], pl.multiple_of(lane + FOLD, 128), imag[q])
            return 0

        lax.fori_loop(0, 8, fold, 0)

    def dft(data, table):
        prod = jnp.dot(data, table, preferred_element_type=jnp.float32)
        return prod[:ST, :128] + (prod[:ST, 128:] + prod[ST:, :128])

    t_copies[0].wait()
    t_copies[1].wait()
    t_copies[2].start()
    power = jnp.zeros((8, ST), jnp.float32)
    for q in range(8):
        if q < 7:
            value = dft(fodd[q], odd_v[1024 * q : 1024 * q + 1024])
        else:
            first_half = lax.rem(lax.broadcasted_iota(jnp.int32, (ST, 128), 1), 64) < 32
            value = jnp.where(first_half, dft(feven[0], even_v[...]), dft(feven[1], even_v[...]))
        value = jnp.transpose(value)
        spec[128 * q : 128 * q + 128, :] = value
        power = power + jnp.sum((value * value).reshape(16, 8, ST), axis=0)
    mean = jnp.sum(power, axis=0, keepdims=True) * (1.0 / BANDS)
    inverse = 1.0 / jnp.sqrt(mean + 1e-06)
    def whiten(s):
        for q in range(8):
            first = 128 * q + 64 * s
            white = (spec[first : first + 64, :] * inverse).astype(jnp.bfloat16)
            asend[s][32 * q : 32 * q + 32] = white.reshape(32, 2, ST)

    whiten(0)
    pl.semaphore_wait(barrier, ALL - 1)

    for s in range(2):
        if s == 1:
            whiten(1)
        to_others(lambda z, w, s=s: send(asend[s].at[w * STA + z], arecv[s].at[me], s, a_sem.at[s], z, w))
        if s == 0:
            for offset in range(1, STA):
                send(pair_ref, pairs.at[me_s], 4, p_sem, column(offset), me_w)
        arecv[s][me] = asend[s][me_w * STA + me_s]
    pairs[me_s, 0, 0] = pair_ref[0, 0]
    pairs[me_s, 0, 1] = pair_ref[0, 1]

    left_lanes = lax.broadcasted_iota(jnp.int32, (WIN, ST), 1) < 64

    def cross(p, s):
        a = pairs[p, 0, 0]
        b = pairs[p, 0, 1]
        a_odd = lax.rem(a, 2) == 1
        b_odd = lax.rem(b, 2) == 1
        left = bands[s, a // 2]
        second = bands[s, b // 2].astype(jnp.float32)
        re, im = second[:WIN], second[WIN:]
        re_roll, im_roll = pltpu.roll(re, 64, 1), pltpu.roll(im, 64, 1)
        re_l, im_l = jnp.where(b_odd, re_roll, re), jnp.where(b_odd, im_roll, im)
        re_r, im_r = jnp.where(b_odd, re, re_roll), jnp.where(b_odd, im, im_roll)
        right = jnp.concatenate(
            [jnp.where(left_lanes, re_l, -im_r), jnp.where(left_lanes, im_l, re_r)], axis=0
        ).astype(jnp.bfloat16)
        prod = lax.dot_general(left, right, (((0,), (0,)), ((), ())), preferred_element_type=jnp.float32)
        prod = jnp.where(a_odd, prod[64:], prod[:64])
        top, low = prod[:32], prod[32:]
        return jnp.where(left_lanes, top, pltpu.roll(low, 64, 1)), jnp.where(left_lanes, pltpu.roll(top, 64, 1), low)

    def encode(p, s, parts):
        largest = jnp.maximum(jnp.abs(parts[0]), jnp.abs(parts[1]))
        exponent = jnp.floor(jnp.log(jnp.maximum(largest, 1e-30)) * (1.0 / math.log(2.0))) + 1.0
        scale = jnp.exp2(11.0 - exponent)
        exponent = exponent.astype(jnp.int32) + 128
        for c, v in enumerate(parts):
            value = jnp.clip(jnp.round(v * scale), -2047.0, 2047.0).astype(jnp.int32)
            codes[pl.ds(c, WIN, stride=2), :] = value * 16 + (jnp.right_shift(exponent, 4 * c) & 15)
        csend[s][pl.ds(WIN * p, WIN)] = codes[:64, :].astype(jnp.int16).reshape(WIN, 2, ST)

    for s in range(2):
        wait(arecv[s].at[pl.ds(0, ALL - 1)], a_sem.at[s])
        for z in range(STA):
            part = arecv[s][WIN * z : WIN * z + WIN].astype(jnp.float32)
            rows[64 * z : 64 * z + 64, :] = part.reshape(2 * WIN, ST)
        for z in range(STA):
            for c in range(2):
                part = rows[pl.ds(64 * z + c, WIN, stride=2), :]
                bands[s, z, WIN * c : WIN * c + WIN, :] = part.astype(jnp.bfloat16)
        if s == 0:
            wait(pairs.at[pl.ds(0, STA - 1)], p_sem)
        for offsets in FAR_FIRST:
            pairs_now = [column(offset) for offset in offsets]
            for p in pairs_now:
                encode(p, s, cross(p, s))

            in_columns(
                offsets, lambda p, w, s=s: send(csend[s].at[p * WIN + w], crecv[s].at[me], 2 + s, c_sem.at[s], p, w)
            )
        crecv[s][me] = csend[s][me]

    t_copies[2].wait()
    wait(pairs.at[pl.ds(0, STA - 1)], send_sem.at[4])
    for s in range(2):
        wait(asend[s].at[pl.ds(0, ALL - 1)], send_sem.at[s])

    for s in range(2):
        wait(crecv[s].at[pl.ds(0, ALL - 1)], c_sem.at[s])
        for z in range(STA):
            part = crecv[s][WIN * z : WIN * z + WIN].astype(jnp.int32)
            codes[64 * z : 64 * z + 64, :] = part.reshape(2 * WIN, ST)
        coded = [codes[pl.ds(c, ALL, stride=2), :] for c in range(2)]
        exponent = (coded[0] & 15) | jnp.left_shift(coded[1] & 15, 4)
        scale = jnp.exp2((exponent - 139).astype(jnp.float32))
        value = jnp.concatenate([jnp.right_shift(v, 4).astype(jnp.float32) * scale for v in coded], axis=0)
        high = value.astype(jnp.bfloat16)
        low = (value - high.astype(jnp.float32)).astype(jnp.bfloat16)
        both = jnp.concatenate([high, low], axis=1)

        for t in range(LAGS // 128):
            row = 128 * t
            value = jnp.zeros((128, 2 * ST), jnp.float32)
            extra = jnp.zeros((128, ST), jnp.float32)
            for block in range(2):
                first = 2 * LAGS * (2 * s + block) + row
                part = both[256 * block : 256 * block + 256]
                value += jnp.dot(lag_v[first : first + 128, :], part, preferred_element_type=jnp.float32)
                extra += jnp.dot(
                    lag_v[first + LAGS : first + LAGS + 128, :], part[:, :ST], preferred_element_type=jnp.float32
                )
            value = value[:, :ST] + (value[:, ST:] + extra)
            if s == 0:
                total[row : row + 128, :] = value
                continue
            value = jnp.transpose(value + total[row : row + 128, :])
            for i2 in range(2):
                for j2 in range(2):
                    part = value[(2 * i2 + j2) * 32 : (2 * i2 + j2) * 32 + 32]
                    order[pl.ds(row + i2 * 64 + j2, 32, stride=2), :] = part
            out_ref[:, :, row : row + 128] = order[row : row + 128, :].reshape(2, 64, 128)
        wait(csend[s].at[pl.ds(0, ALL - 1)], send_sem.at[2 + s])


def body(traces, pair_blocks):
    table = jnp.asarray(tables())
    f32, bf16, i16 = jnp.float32, jnp.bfloat16, jnp.int16
    hbm = pl.BlockSpec(memory_space=pltpu.HBM)
    out = pl.pallas_call(
        kernel,
        out_shape=jax.ShapeDtypeStruct((2, 64, LAGS), f32),
        in_specs=[hbm, pl.BlockSpec(memory_space=pltpu.SMEM), hbm],
        out_specs=pl.BlockSpec(memory_space=pltpu.VMEM),
        scratch_shapes=[
            pltpu.VMEM((ST * SEG, 128), f32),
            pltpu.VMEM((ODD, 256), bf16),
            pltpu.VMEM((FOLD, 256), bf16),
            pltpu.VMEM((8 * LAGS, 256), bf16),
            pltpu.SMEM((STA, 1, 2), jnp.int32),
            pltpu.VMEM((7, 2 * ST, 2 * FOLD), bf16),
            pltpu.VMEM((2, 2 * ST, FOLD), bf16),
            pltpu.VMEM((2 * BANDS, ST), f32),
            pltpu.VMEM((BANDS, ST), f32),
            pltpu.VMEM((2, STA, 2 * WIN, ST), bf16),
            pltpu.VMEM((BANDS, ST), jnp.int32),
            pltpu.VMEM((LAGS, ST), f32),
            pltpu.VMEM((LAGS, ST), f32),
        ]
        + [pltpu.VMEM((ALL, 2, ST), bf16)] * 4
        + [pltpu.VMEM((ALL, 2, ST), i16)] * 4
        + [
            pltpu.SemaphoreType.DMA((4,)),
            pltpu.SemaphoreType.DMA((3,)),
            pltpu.SemaphoreType.DMA((5,)),
            pltpu.SemaphoreType.DMA,
            pltpu.SemaphoreType.DMA((2,)),
            pltpu.SemaphoreType.DMA((2,)),
        ],
        compiler_params=pltpu.CompilerParams(
            collective_id=0, has_side_effects=True, vmem_limit_bytes=52 * 1024 * 1024
        ),
        name="noise_correlation",
    )(traces.reshape(ST * SEG, 128), pair_blocks, table)
    return out.reshape(2, 1, 64, LAGS)


def solution(mesh):
    in_specs = (P("sta", "win", None), P("sta", None))
    out_specs = P("win", "sta", None, None)
    return jax.shard_map(body, mesh=mesh, in_specs=in_specs, out_specs=out_specs, check_vma=False)
```
